256 devices in a mesh: dp: 4 (over x), ctx: 64 (over z, y, core).
Axes of the slice: x: 4, y: 4, z: 8, core: 2. Of those that a mesh axis runs over, the one named last changes fastest.
Arguments:
- query_in: bfloat16 [4, 16384, 2048], P('dp', 'ctx'), may hold values from -68 to 68
- key_in: bfloat16 [4, 16384, 2048], P('dp', 'ctx'), may hold values from -6 to 6
- value_in: bfloat16 [4, 16384, 2048], P('dp', 'ctx'), may hold values from -6 to 6
- conv_weight: float32 [3, 4, 2048], replicated, may hold values from -3 to 3
- out_grad: bfloat16 [4, 16384, 2048], P('dp', 'ctx'), may hold values from -6 to 6
- block_lists: int32 [4, 256, 16], P('dp', 'ctx'), may hold values from 0 to 255, as said below
Outputs:
- query_in_grad: bfloat16 [4, 16384, 2048], P('dp', 'ctx')
- key_in_grad: bfloat16 [4, 16384, 2048], P('dp', 'ctx')
- value_in_grad: bfloat16 [4, 16384, 2048], P('dp', 'ctx')
- conv_grad: float32 [3, 4, 2048], replicated
The draws below stay inside these ranges and needn't reach their ends.
Inputs may be any that keep to these rules, and one draw needn't show every extreme that they name: `block_lists`: entry n names key block n of the sequence. Each list names the 1 key block of its own query block and no block twice. The lists in the rows of ctx index i name only blocks held by ctx index i or by ctx indices (i - d) mod 64 for d = 1 to 6, and at most 2 distinct blocks held by any one other index; this most is reached.
All inputs are finite; a program needn't handle non-finite values.
Results may differ from the reference program's by a relative error of at most 0.012.
The reference program's roundings to bfloat16 on the way count: a program that leaves them out, or rounds other values in their place, can miss the bound.
Values may be sent and summed in bfloat16 or wider, within the bound.
No kernel may reach another device: no remote copies, remote signals or barrier semaphores. Data moves between devices by JAX's collectives and lax.ppermute only.
A program may use at most 192 MiB of HBM per device.

```python
import math
import jax
import jax.numpy as jnp
from jax import lax

HEADS = 16
HEAD = 128
TAPS = 4
QBLK = 64
KBLK = 64
SEL = 16
DEVICES_BEHIND = 6
MAX_REMOTE_KEYS = 2
TOK_DEV = 256
SEQS = 4
SEQ_LEN = 16384
N_CTX = 64


def draw_query_in(key, part):
    key = jax.random.fold_in(key, 3)
    shape = (SEQS, SEQ_LEN, HEADS * HEAD)
    return jax.random.truncated_normal(key, -6.0, 6.0, shape, jnp.float32).astype(jnp.bfloat16)


def draw_block_lists(key, part):
    key = jax.random.fold_in(key, 7)
    group_width = N_CTX
    half_rows = TOK_DEV // 2
    blocks_half = half_rows // KBLK
    blocks_per_device = 2 * blocks_half
    queries_half = half_rows // QBLK
    queries_dev = 2 * queries_half
    own_count = QBLK // KBLK
    pick_count = SEL - own_count
    remote_count = DEVICES_BEHIND * MAX_REMOTE_KEYS
    width_all = blocks_per_device + remote_count

    def one_sequence(seq_key):
        key_choice, key_popular, key_noise = jax.random.split(seq_key, 3)
        random_rank = jax.random.randint(key_choice, (group_width, DEVICES_BEHIND, blocks_per_device), 0, 1 << 16)
        ranked = random_rank * blocks_per_device + jnp.arange(blocks_per_device, dtype=jnp.int32)
        _, chosen = lax.top_k(ranked, MAX_REMOTE_KEYS)
        device_ids = jnp.arange(group_width, dtype=jnp.int32)
        reach_ids = jnp.arange(1, DEVICES_BEHIND + 1, dtype=jnp.int32)
        owner_ids = ((device_ids[:, None] - reach_ids[None, :]) % group_width)[:, :, None]
        span_ids = jnp.where(chosen < blocks_half, owner_ids, 2 * group_width - 1 - owner_ids)
        remote_pos = (span_ids * blocks_half + chosen % blocks_half).reshape(group_width, remote_count)
        local_ids = jnp.arange(blocks_per_device, dtype=jnp.int32)[None, :]
        own_span = jnp.where(local_ids < blocks_half, device_ids[:, None], 2 * group_width - 1 - device_ids[:, None])
        own_pos = own_span * blocks_half + local_ids % blocks_half
        block_pos = jnp.concatenate([own_pos, remote_pos], axis=1)
        popular_boost = jnp.repeat(jnp.where(jax.random.randint(key_popular, (group_width, DEVICES_BEHIND), 0, 8) == 0, 2048, 0), MAX_REMOTE_KEYS, axis=1)
        popular_boost = jnp.concatenate([jnp.zeros((group_width, blocks_per_device), jnp.int32), popular_boost], axis=1)
        random_jitter = jax.random.randint(key_noise, (group_width, queries_dev, width_all), 0, 1024)
        row_ids = jnp.arange(queries_dev, dtype=jnp.int32)[None, :]
        query_span = jnp.where(row_ids < queries_half, device_ids[:, None], 2 * group_width - 1 - device_ids[:, None])
        first_block = (query_span * queries_half + row_ids % queries_half) * own_count
        candidates = jnp.broadcast_to(block_pos[:, None, :], (group_width, queries_dev, width_all))
        gap = candidates - first_block[:, :, None]
        causal_only = (gap < 0).astype(jnp.int32)
        close_blocks = (jnp.abs(gap) < 4 * own_count).astype(jnp.int32)
        remote_col = (jnp.arange(width_all, dtype=jnp.int32) >= blocks_per_device)[None, None, :]
        first_row = (jnp.arange(queries_dev, dtype=jnp.int32) == 0)[None, :, None]
        block_rating = random_jitter + 4096 * causal_only + 1024 * close_blocks + popular_boost[:, None, :]
        block_rating = block_rating + jnp.where(remote_col & first_row, 16384, 0)
        own_mask = (gap >= 0) & (gap < own_count)
        block_rating = jnp.where(own_mask, -(1 << 20), block_rating)
        flat_score = block_rating * width_all + jnp.arange(width_all, dtype=jnp.int32)
        _, picked_index = lax.top_k(flat_score, pick_count)
        picked = jnp.take_along_axis(candidates, picked_index, axis=2)
        own_blocks = first_block[:, :, None] + jnp.arange(own_count, dtype=jnp.int32)[None, None, :]
        lists = jnp.concatenate([own_blocks, picked], axis=2)
        return lists.reshape(group_width * queries_dev, SEL).astype(jnp.int32)
    seq_keys = jax.random.split(key, SEQS)
    return jax.vmap(one_sequence)(seq_keys)


def shard_levels(stream_key, dims, shards, least, high):
    loudness, own = 1.0, jax.random.fold_in(stream_key, 6)
    for position, shards_of in shards:
        draws = jnp.exp(jax.random.uniform(jax.random.fold_in(own, position), (shards_of,), jnp.float32, least / len(shards), high / len(shards)))
        loudness = loudness * jnp.repeat(draws, dims[position] // shards_of).reshape([-1 if axis == position else 1 for axis in range(len(dims))])
    return loudness


def noise(stream_key, extent, width, reach, shards=(), kind=jnp.bfloat16):
    gain = shard_levels(stream_key, extent, shards, -0.22, 0.18) if shards else 1.0
    values = jax.random.normal(stream_key, extent, jnp.float32) * width * gain
    return jnp.minimum(jnp.maximum(values, -reach), reach).astype(kind)


def setup_inputs(seed: int = 0) -> dict:
    key_of = jax.random.split(jax.random.key(seed), 7)
    query_in = draw_query_in(jax.random.fold_in(key_of[6], 71), 0)
    key_in = noise(key_of[1], (SEQS, SEQ_LEN, HEADS * HEAD), 1.0, 6.0, ((0, 4), (1, 64)))
    value_in = noise(key_of[2], (SEQS, SEQ_LEN, HEADS * HEAD), 1.0, 6.0, ((0, 4), (1, 64)))
    conv_weight = noise(key_of[3], (3, TAPS, HEADS * HEAD), TAPS ** -0.5, 3.0, (), jnp.float32)
    out_grad = noise(key_of[4], (SEQS, SEQ_LEN, HEADS * HEAD), 1.0, 6.0, ((0, 4), (1, 64)))
    block_lists = draw_block_lists(jax.random.fold_in(key_of[6], 71), 0)
    return {"query_in": query_in, "key_in": key_in, "value_in": value_in, "conv_weight": conv_weight, "out_grad": out_grad, "block_lists": block_lists}


def unstore(stored):
    trailing = stored.shape[1:]
    shaped = stored.reshape((N_CTX, 2, stored.shape[0] // (2 * N_CTX)) + trailing)
    return jnp.concatenate([shaped[:, 0].reshape((-1,) + trailing), shaped[::-1, 1].reshape((-1,) + trailing)], axis=0)


def restore(ordered):
    middle = ordered.shape[0] // 2
    trailing = ordered.shape[1:]
    lower_half = ordered[:middle].reshape((N_CTX, -1) + trailing)
    upper_half = ordered[middle:].reshape((N_CTX, -1) + trailing)[::-1]
    return jnp.stack([lower_half, upper_half], axis=1).reshape(ordered.shape)


def half_round(values):
    return lax.optimization_barrier(values.astype(jnp.bfloat16)).astype(jnp.float32)


def conv_forward(inputs, weight):
    length = inputs.shape[0]
    padded = jnp.pad(inputs.astype(jnp.float32), ((TAPS - 1, 0), (0, 0)))
    result = weight[0] * padded[TAPS - 1:TAPS - 1 + length]
    for offset in range(1, TAPS):
        result = result + weight[offset] * padded[TAPS - 1 - offset:TAPS - 1 - offset + length]
    return result


def conv_backward(grad_rows, inputs, weight):
    length = grad_rows.shape[0]
    padded_after = jnp.pad(grad_rows, ((0, TAPS - 1), (0, 0)))
    before = jnp.pad(inputs.astype(jnp.float32), ((TAPS - 1, 0), (0, 0)))
    result = weight[0] * padded_after[:length]
    tap_terms = [jnp.sum(grad_rows * before[TAPS - 1:TAPS - 1 + length], axis=0)]
    for offset in range(1, TAPS):
        result = result + weight[offset] * padded_after[offset:offset + length]
        tap_terms.append(jnp.sum(grad_rows * before[TAPS - 1 - offset:TAPS - 1 - offset + length], axis=0))
    return result.astype(jnp.bfloat16), jnp.stack(tap_terms)


def block_grads(queries, key_rows, value_rows, cotangent, query_pos, key_pos):
    block_count = queries.shape[0]
    head_count = queries.shape[-1] // HEAD
    scale_factor = HEAD ** -0.5
    query_heads = queries.astype(jnp.float32).reshape(block_count, -1, head_count, HEAD)
    key_heads = key_rows.astype(jnp.float32).reshape(block_count, -1, head_count, HEAD)
    value_heads = value_rows.astype(jnp.float32).reshape(block_count, -1, head_count, HEAD)
    grad_heads = cotangent.astype(jnp.float32).reshape(block_count, -1, head_count, HEAD)
    scores = jnp.einsum('nqhd,nkhd->nhqk', query_heads, key_heads) * scale_factor
    visible = key_pos[:, None, None, :] <= query_pos[:, None, :, None]
    scores = jnp.where(visible, scores, -jnp.inf)
    row_max = jnp.max(scores, axis=-1, keepdims=True)
    log_total = row_max + jnp.log(jnp.sum(jnp.exp(scores - row_max), axis=-1, keepdims=True))
    attn_probs = jnp.where(visible, jnp.exp(scores - log_total), 0.0)
    probs_half = half_round(attn_probs)
    outputs = jnp.einsum('nhqk,nkhd->nqhd', probs_half, value_heads)
    delta_rows = jnp.sum(outputs * grad_heads, axis=-1)
    prob_grads = jnp.einsum('nqhd,nkhd->nhqk', grad_heads, value_heads)
    score_grads = half_round(attn_probs * (prob_grads - jnp.transpose(delta_rows, (0, 2, 1))[..., None]))
    query_grads = jnp.einsum('nhqk,nkhd->nqhd', score_grads, key_heads) * scale_factor
    key_terms = jnp.einsum('nhqk,nqhd->nkhd', score_grads, query_heads) * scale_factor
    value_terms = jnp.einsum('nhqk,nqhd->nkhd', probs_half, grad_heads)
    channels = queries.shape[-1]
    return (query_grads.reshape(block_count, -1, channels), key_terms.reshape(block_count, -1, channels),
            value_terms.reshape(block_count, -1, channels))


def attention_grads(q_field, k_field, v_field, cotangent, lists):
    length = q_field.shape[0]
    channels = q_field.shape[1]
    block_count = length // QBLK
    group_len = math.gcd(block_count, 8)
    step_count = block_count // group_len

    def scan_step(carried, which):
        key_acc, value_acc = carried
        blocks = which * group_len + jnp.arange(group_len, dtype=jnp.int32)
        query_rows = blocks[:, None] * QBLK + jnp.arange(QBLK, dtype=jnp.int32)[None, :]
        entries = jnp.take(lists, blocks, axis=0).astype(jnp.int32)
        key_rows = (entries[:, :, None] * KBLK + jnp.arange(KBLK, dtype=jnp.int32)[None, None, :]).reshape(group_len, -1)
        query_grads, key_terms, value_terms = block_grads(
            jnp.take(q_field, query_rows, axis=0), jnp.take(k_field, key_rows, axis=0),
            jnp.take(v_field, key_rows, axis=0), jnp.take(cotangent, query_rows, axis=0), query_rows, key_rows)
        flat_rows = key_rows.reshape(-1)
        key_acc = key_acc.at[flat_rows].add(key_terms.reshape(-1, channels))
        value_acc = value_acc.at[flat_rows].add(value_terms.reshape(-1, channels))
        return (key_acc, value_acc), query_grads

    empty_grads = jnp.zeros((length, channels), jnp.float32)
    (key_grads, value_grads), query_grads = lax.scan(scan_step, (empty_grads, empty_grads), jnp.arange(step_count, dtype=jnp.int32))
    return query_grads.reshape(length, channels), key_grads, value_grads


def reference(query_in, key_in, value_in, conv_weight, out_grad, block_lists):
    def one_sequence(arrays):
        q_raw, k_raw, v_raw, cotangent, lists = arrays
        ordered_in = [unstore(q_raw), unstore(k_raw), unstore(v_raw)]
        fields = [conv_forward(ordered_in[slot_no], conv_weight[slot_no]).astype(jnp.bfloat16) for slot_no in range(3)]
        grads_all = attention_grads(fields[0], fields[1], fields[2], unstore(cotangent), unstore(lists))
        results = []
        weight_terms = []
        for slot_no in range(3):
            grad_input, tap_terms = conv_backward(grads_all[slot_no], ordered_in[slot_no], conv_weight[slot_no])
            results.append(restore(grad_input))
            weight_terms.append(tap_terms)
        return results[0], results[1], results[2], jnp.stack(weight_terms)

    query_grad, key_grad, value_grad, kernel_terms = lax.map(one_sequence, (query_in, key_in, value_in, out_grad, block_lists))
    return query_grad, key_grad, value_grad, jnp.sum(kernel_terms, axis=0)
```

```python
import math

import jax
import jax.numpy as jnp
from jax import lax
from jax.sharding import PartitionSpec as P

HEAD = 128
TAPS = 4
QBLK = 64
KBLK = 64
DEVICES_BEHIND = 6
MAX_REMOTE_KEYS = 2


def with_halo(x, sides, width):
    for axis, dim in sides:
        count, length = (lax.axis_size(axis), x.shape[dim])
        up = [(i, (i + 1) % count) for i in range(count - 1)]
        down = [(j, i) for i, j in up]
        last = lax.slice_in_dim(x, length - width, length, axis=dim)
        leading = lax.slice_in_dim(x, 0, width, axis=dim)
        before = lax.ppermute(last, axis, up)
        after = lax.ppermute(leading, axis, down)
        x = jnp.concatenate([before, x, after], axis=dim)
    return x


def passed_along(x, axis, by):
    count = lax.axis_size(axis)
    return lax.ppermute(x, axis, [(i, (i + by) % count) for i in range(count)])


def summed_over(x, axis):
    count = lax.axis_size(axis)
    step = 1
    while step < count:
        x = x + lax.ppermute(x, axis, [(i, i ^ step) for i in range(count)])
        step *= 2
    return x


def for_sending(x):
    return jax.tree.map(lambda a: a.astype(jnp.bfloat16) if a.dtype == jnp.float32 else a, x)


def locate(lists, half_rows, group_width):
    span_index = lists * KBLK // half_rows
    upper_mask = span_index >= group_width
    owners = jnp.where(upper_mask, 2 * group_width - 1 - span_index, span_index)
    local_index = (
        jnp.where(upper_mask, half_rows // KBLK, 0)
        + (lists * KBLK - span_index * half_rows) // KBLK
    )
    return (owners, local_index)


def pick_slots(wanted, slot_cap):
    slot_rank = jnp.cumsum(wanted.astype(jnp.int32), axis=1) - 1
    block_ids = jnp.arange(wanted.shape[1], dtype=jnp.int32)
    hits = wanted[:, :, None] & (
        slot_rank[:, :, None] == jnp.arange(slot_cap, dtype=jnp.int32)[None, None, :]
    )
    chosen = jnp.sum(jnp.where(hits, block_ids[None, :, None], 0), axis=1)
    return (jnp.where(jnp.any(hits, axis=1), chosen, -1), slot_rank)


def convolve(extended, weight, length):
    rim_rows = TAPS - 1
    result = weight[:, 0, None, :] * extended[:, rim_rows : rim_rows + length]
    for offset in range(1, TAPS):
        result = (
            result
            + weight[:, offset, None, :]
            * extended[:, rim_rows - offset : rim_rows - offset + length]
        )
    return result


def unconvolve(extended, weight, length):
    result = weight[:, 0, None, :] * extended[:, :length]
    for offset in range(1, TAPS):
        result = result + weight[:, offset, None, :] * extended[:, offset : offset + length]
    return result


def tap_sums(grad_rows, extended):
    length = grad_rows.shape[1]
    rim_rows = TAPS - 1
    return jnp.stack(
        [
            jnp.sum(grad_rows * extended[:, rim_rows - offset : rim_rows - offset + length], axis=1)
            for offset in range(TAPS)
        ],
        axis=1,
    )


def body(query_in, key_in, value_in, conv_weight, out_grad, block_lists):
    stacked = jnp.stack([query_in[0], key_in[0], value_in[0]])
    tok_rows = stacked.shape[1]
    half_rows = tok_rows // 2
    channels = stacked.shape[2]
    rim_rows = TAPS - 1
    group_width = lax.axis_size("ctx")
    my_index = lax.axis_index("ctx")
    is_last = my_index == group_width - 1
    edge_rows = jnp.concatenate(
        [stacked[:, tok_rows - rim_rows :], stacked[:, half_rows - rim_rows : half_rows]], axis=1
    )
    edged = with_halo(edge_rows, (("ctx", 1),), rim_rows)
    before_low = edged[:, :rim_rows]
    before_high = jnp.where(
        is_last, stacked[:, half_rows - rim_rows : half_rows], edged[:, 3 * rim_rows :]
    )
    extended_low = jnp.concatenate([before_low, stacked[:, :half_rows]], axis=1).astype(jnp.float32)
    extended_high = jnp.concatenate([before_high, stacked[:, half_rows:]], axis=1).astype(
        jnp.float32
    )
    fields = jnp.concatenate(
        [
            convolve(extended_low, conv_weight, half_rows),
            convolve(extended_high, conv_weight, half_rows),
        ],
        axis=1,
    ).astype(jnp.bfloat16)
    spread = jnp.arange(half_rows, dtype=jnp.int32)
    positions = jnp.concatenate(
        [my_index * half_rows + spread, (2 * group_width - 1 - my_index) * half_rows + spread]
    )
    lists = block_lists[0]
    key_blocks = tok_rows // KBLK
    remote_slots = DEVICES_BEHIND * MAX_REMOTE_KEYS
    slots_total = remote_slots + key_blocks
    block_ids = jnp.arange(key_blocks, dtype=jnp.int32)
    owners, local_index = locate(lists, half_rows, group_width)
    distance = (my_index - owners) % group_width
    remote_mask = owners != my_index
    reach_ids = jnp.arange(1, DEVICES_BEHIND + 1, dtype=jnp.int32)
    match_reach = (distance.reshape(-1)[:, None] == reach_ids[None, :]) & remote_mask.reshape(-1)[
        :, None
    ]
    match_block = local_index.reshape(-1)[:, None] == block_ids[None, :]
    wanted = jnp.any(match_reach[:, :, None] & match_block[:, None, :], axis=0)
    requested, slot_rank = pick_slots(wanted, MAX_REMOTE_KEYS)
    reach_row = jnp.maximum(distance - 1, 0)
    slot_index = reach_row * MAX_REMOTE_KEYS + slot_rank[reach_row, local_index]
    table_index = jnp.where(remote_mask, slot_index, remote_slots + local_index)
    local_keys = fields[1].reshape(key_blocks, KBLK, channels)
    local_values = fields[2].reshape(key_blocks, KBLK, channels)
    served_rows = []
    fetched_keys = []
    fetched_values = []
    for reach_step in range(1, DEVICES_BEHIND + 1):
        served = passed_along(requested[reach_step - 1], "ctx", -reach_step)
        pick_rows = jnp.maximum(served, 0)
        got_keys, got_values = passed_along(
            (local_keys[pick_rows], local_values[pick_rows]), "ctx", reach_step
        )
        served_rows.append(served)
        fetched_keys.append(got_keys)
        fetched_values.append(got_values)
    served_all = jnp.stack(served_rows)
    head_count = channels // HEAD
    key_table = jnp.concatenate(
        [jnp.stack(fetched_keys).reshape(remote_slots * KBLK, channels), fields[1]], axis=0
    ).reshape(-1, head_count, HEAD)
    value_table = jnp.concatenate(
        [jnp.stack(fetched_values).reshape(remote_slots * KBLK, channels), fields[2]], axis=0
    ).reshape(-1, head_count, HEAD)
    scale_factor = HEAD ** (-0.5)
    slot_match = table_index[:, :, None] == jnp.arange(slots_total, dtype=jnp.int32)[None, None, :]
    member = jnp.any(slot_match, axis=1)
    slot_block = jnp.max(jnp.where(slot_match, lists[:, :, None], -1), axis=(0, 1))
    key_pos = (slot_block[:, None] * KBLK + jnp.arange(KBLK, dtype=jnp.int32)[None, :]).reshape(-1)
    named = jnp.repeat(jnp.repeat(member, QBLK, axis=0), KBLK, axis=1)
    visible = named & (key_pos[None, :] <= positions[:, None])
    query_heads = fields[0].reshape(tok_rows, head_count, HEAD)
    grad_heads = out_grad[0].reshape(tok_rows, head_count, HEAD)
    group_heads = math.gcd(head_count, 8)
    group_count = head_count // group_heads

    def as_slots(pieces):
        return jnp.concatenate(pieces, axis=1).reshape(slots_total, KBLK * channels)

    value_pieces = []
    query_pieces = []
    key_pieces = []
    for group_no in range(group_count):
        probabilities_first = group_no * group_heads
        probabilities_last = probabilities_first + group_heads
        scores = (
            jnp.einsum(
                "qhd,khd->hqk",
                query_heads[:, probabilities_first:probabilities_last],
                key_table[:, probabilities_first:probabilities_last],
                preferred_element_type=jnp.float32,
            )
            * scale_factor
        )
        scores = jnp.where(visible[None], scores, -jnp.inf)
        row_max = jnp.max(scores, axis=-1, keepdims=True)
        log_total = row_max + jnp.log(jnp.sum(jnp.exp(scores - row_max), axis=-1, keepdims=True))
        attn_probs = jnp.where(visible[None], jnp.exp(scores - log_total), 0.0)
        value_first = group_no * group_heads
        value_last = value_first + group_heads
        value_probs_half = attn_probs.astype(jnp.bfloat16)
        value_pieces.append(
            jnp.einsum(
                "hqk,qhd->khd",
                value_probs_half,
                grad_heads[:, value_first:value_last],
                preferred_element_type=jnp.float32,
            )
        )
        first = group_no * group_heads
        last = first + group_heads
        probs_half = attn_probs.astype(jnp.bfloat16)
        value_rows = value_table[:, first:last]
        key_rows = key_table[:, first:last]
        grads_here = grad_heads[:, first:last]
        outputs = jnp.einsum(
            "hqk,khd->qhd", probs_half, value_rows, preferred_element_type=jnp.float32
        )
        delta_rows = jnp.sum(outputs * grads_here.astype(jnp.float32), axis=-1)
        prob_grads = jnp.einsum(
            "qhd,khd->hqk", grads_here, value_rows, preferred_element_type=jnp.float32
        )
        score_grads = (
            attn_probs * (prob_grads - jnp.transpose(delta_rows, (1, 0))[..., None])
        ).astype(jnp.bfloat16)
        query_grads = (
            jnp.einsum("hqk,khd->qhd", score_grads, key_rows, preferred_element_type=jnp.float32)
            * scale_factor
        )
        key_terms = (
            jnp.einsum(
                "hqk,qhd->khd",
                score_grads,
                query_heads[:, first:last],
                preferred_element_type=jnp.float32,
            )
            * scale_factor
        )
        query_grads, key_terms = (query_grads, key_terms)
        query_pieces.append(query_grads)
        key_pieces.append(key_terms)
    value_slots = as_slots(value_pieces)
    key_slots = as_slots(key_pieces)
    query_all = jnp.concatenate(query_pieces, axis=1)
    key_out = key_slots[:remote_slots].reshape(DEVICES_BEHIND, MAX_REMOTE_KEYS, -1)
    value_out = value_slots[:remote_slots].reshape(DEVICES_BEHIND, MAX_REMOTE_KEYS, -1)
    key_parts = []
    value_parts = []
    for reach_step in range(1, DEVICES_BEHIND + 1):
        key_piece, value_piece = (
            passed_along(key_out[reach_step - 1].astype(jnp.bfloat16), "ctx", -reach_step).astype(
                jnp.float32
            ),
            passed_along(value_out[reach_step - 1].astype(jnp.bfloat16), "ctx", -reach_step).astype(
                jnp.float32
            ),
        )
        key_parts.append(key_piece)
        value_parts.append(value_piece)
    key_back = jnp.stack(key_parts)
    value_back = jnp.stack(value_parts)
    targets = jnp.where(served_all >= 0, served_all, key_blocks).reshape(-1)

    def placed_terms(back):
        rows = back.reshape(remote_slots, -1)
        sums = []
        for block in range(key_blocks):
            total = jnp.where(targets[0] == block, rows[0], 0.0)
            for slot in range(1, remote_slots):
                total = total + jnp.where(targets[slot] == block, rows[slot], 0.0)
            sums.append(total)
        return jnp.stack(sums)

    key_recv = placed_terms(key_back)
    value_recv = placed_terms(value_back)
    key_grads = (key_slots[remote_slots:] + key_recv).reshape(tok_rows, channels)
    value_grads = (value_slots[remote_slots:] + value_recv).reshape(tok_rows, channels)
    grad_rows = jnp.stack([query_all.reshape(tok_rows, channels), key_grads, value_grads])
    grad_edge = jnp.concatenate(
        [grad_rows[:, :rim_rows], grad_rows[:, half_rows : half_rows + rim_rows]], axis=1
    )
    grad_edged = with_halo(for_sending(grad_edge), (("ctx", 1),), rim_rows).astype(grad_edge.dtype)
    after_high = grad_edged[:, :rim_rows]
    after_low = jnp.where(
        is_last, grad_rows[:, half_rows : half_rows + rim_rows], grad_edged[:, 3 * rim_rows :]
    )
    grad_low = jnp.concatenate([grad_rows[:, :half_rows], after_low], axis=1)
    grad_high = jnp.concatenate([grad_rows[:, half_rows:], after_high], axis=1)
    input_grads = jnp.concatenate(
        [
            unconvolve(grad_low, conv_weight, half_rows),
            unconvolve(grad_high, conv_weight, half_rows),
        ],
        axis=1,
    ).astype(jnp.bfloat16)
    kernel_terms = tap_sums(grad_rows[:, :half_rows], extended_low) + tap_sums(
        grad_rows[:, half_rows:], extended_high
    )
    kernel_grad = summed_over(summed_over(kernel_terms, "ctx"), "dp")
    return (input_grads[0][None], input_grads[1][None], input_grads[2][None], kernel_grad)


def solution(mesh):
    placed = (
        P("dp", "ctx", None),
        P("dp", "ctx", None),
        P("dp", "ctx", None),
        P(),
        P("dp", "ctx", None),
        P("dp", "ctx", None),
    )
    return jax.shard_map(
        body,
        mesh=mesh,
        in_specs=placed,
        out_specs=(P("dp", "ctx", None), P("dp", "ctx", None), P("dp", "ctx", None), P()),
        check_vma=False,
    )
```

```python
import functools
import math

import jax
import jax.numpy as jnp
from jax import lax
from jax.experimental import pallas as pl
from jax.experimental.pallas import tpu as pltpu
from jax.sharding import PartitionSpec as P

HEAD = 128
TAPS = 4
BLK = 64
BEHIND = 6
MAX_REMOTE = 2
HALF = 128
OWN_BLOCKS = 4
PAD = 8
RUN = HALF + PAD
SLOTS = BEHIND * MAX_REMOTE
KEYS = SLOTS * BLK + 2 * HALF
GROUPS = 2
HIDDEN = 1 << 30
VMEM = 48 * 1024 * 1024


def along(x, pairs):
    return lax.ppermute(x, "ctx", pairs)


def ring_pairs(count, by):
    return [(i, (i + by) % count) for i in range(count)]


def sibling_pairs(count):
    return [(i, i ^ 1) for i in range(count)]


def wrapped_out(count, by):
    return [(i, i + by - count) for i in range(count - by, count)]


def wrapped_back(count, by):
    return [(j, i) for i, j in wrapped_out(count, by)]


def summed_over(x, axis):
    count = lax.axis_size(axis)
    step = 1
    while step < count:
        x = x + lax.ppermute(x, axis, [(i, i ^ step) for i in range(count)])
        step *= 2
    return x


def shared(own, from_two, from_four, from_six, first_core, pairs):
    mine = jnp.stack(
        [
            jnp.where(first_core, own, from_two),
            jnp.where(first_core, from_two, from_four),
            jnp.where(first_core, from_four, from_six),
        ]
    )
    return along(mine, pairs)


def table_of_slots(lists, my_index, count):
    span = lists * BLK // HALF
    upper = span >= count
    owners = jnp.where(upper, 2 * count - 1 - span, span)
    local = jnp.where(upper, OWN_BLOCKS // 2, 0) + lists % (HALF // BLK)
    distance = ((my_index - owners) % count).reshape(-1)
    reach = BEHIND - jnp.arange(BEHIND, dtype=jnp.int32)
    block_ids = jnp.arange(OWN_BLOCKS, dtype=jnp.int32)
    wanted = jnp.any(
        (distance[:, None, None] == reach[None, :, None])
        & (local.reshape(-1)[:, None, None] == block_ids[None, None, :]),
        axis=0,
    )
    rank = jnp.cumsum(wanted.astype(jnp.int32), axis=1) - 1
    slot_ids = jnp.arange(MAX_REMOTE, dtype=jnp.int32)
    hits = wanted[:, :, None] & (rank[:, :, None] == slot_ids[None, None, :])
    chosen = jnp.sum(jnp.where(hits, block_ids[None, :, None], 0), axis=1)
    chosen_named = jnp.any(hits, axis=1)
    wraps = (reach > my_index)[:, None]
    block = jnp.where(wraps, chosen, slot_ids[None, :])
    named = jnp.where(wraps, chosen_named, wanted[:, :MAX_REMOTE])
    rows = jnp.arange(BEHIND, dtype=jnp.int32)[:, None]
    index = jnp.where(block < 2, rows * 2 + block, SLOTS + rows * 2 + block - 2)
    owner = ((my_index - reach) % count)[:, None]
    piece = jnp.where(block < 2, owner, 2 * count - 1 - owner)
    start = piece * HALF + (block % 2) * BLK
    start = jnp.where(named, start, HIDDEN)
    spread = jnp.arange(BLK, dtype=jnp.int32)
    positions = (start.reshape(-1)[:, None] + spread[None, :]).reshape(-1)
    return index.reshape(-1), positions


def attention_kernel(
    meta, key_pos, query_pos, q_raw, k_raw, v_raw, cot, weight, q_halo, far_halo, high_halo,
    two, four, six, odd, e_two, e_four, e_six, e_odd,
    dq_out, own_out, odd_out, even_out, e_odd_out, e_even_out, taps_out,
    hide, xq, xk, xv, kall, vall, kt, vt, scores, dprob, probs_half, dscore, gk, gv,
):
    my_index = meta[SLOTS]
    wrapping = my_index < BEHIND
    scale = HEAD ** -0.5
    f32 = jnp.float32
    half = jnp.bfloat16

    @pl.when(pl.program_id(0) == 0)
    def _():
        hide[...] = jnp.where(key_pos[...] <= query_pos[...], 0.0, -jnp.inf)
        gk[...] = jnp.zeros_like(gk)
        gv[...] = jnp.zeros_like(gv)

    raw = (xk, xv)
    fields = (kall, vall)
    tables = (kt, vt)
    near = {1: lambda n: odd[0, n], 3: lambda n: odd[1, n], 5: lambda n: odd[2, n],
            2: lambda n: two[n], 4: lambda n: four[n], 6: lambda n: six[n]}
    wrapped = {1: lambda n: e_odd[0, n], 3: lambda n: e_odd[1, n], 5: lambda n: e_odd[2, n],
               2: lambda n: e_two[n], 4: lambda n: e_four[n], 6: lambda n: e_six[n]}

    def convolved(x, place, which):
        base = place * RUN + PAD
        total = weight[which, 0:1, :] * x[base : base + HALF, :]
        for tap in range(1, TAPS):
            total = total + weight[which, tap : tap + 1, :] * x[base - tap : base - tap + HALF, :]
        return total.astype(half)

    def last_rows(x, place):
        return x[place * RUN + HALF : place * RUN + RUN, :]

    for side in range(2):
        xq[side * RUN : side * RUN + PAD, :] = q_halo[side]
        xq[side * RUN + PAD : (side + 1) * RUN, :] = q_raw[side * HALF : (side + 1) * HALF, :].astype(f32)
    queries = jnp.concatenate([convolved(xq, 0, 0), convolved(xq, 1, 0)], axis=0)

    own_raw = (k_raw, v_raw)
    for n in range(2):
        x = raw[n]
        for place in range(BEHIND + 1):
            base = place * RUN
            if place < BEHIND:
                rows = near[BEHIND - place](n).astype(f32)
            else:
                rows = own_raw[n][0:HALF, :].astype(f32)
            before = far_halo[n] if place == 0 else last_rows(x, place - 1)
            x[base : base + PAD, :] = jnp.where(BEHIND - place == my_index, 0.0, before)
            x[base + PAD : base + RUN, :] = rows
        base = (BEHIND + 1) * RUN
        x[base : base + PAD, :] = high_halo[n]
        x[base + PAD : base + RUN, :] = own_raw[n][HALF : 2 * HALF, :].astype(f32)
        for place in range(BEHIND):
            fields[n][place * HALF : (place + 1) * HALF, :] = convolved(x, place, n + 1)
        for side in range(2):
            first = SLOTS * BLK + side * HALF
            tables[n][first : first + HALF, :] = convolved(x, BEHIND + side, n + 1)

    @pl.when(wrapping)
    def _():
        gk[...] = jnp.zeros_like(gk)
        gv[...] = jnp.zeros_like(gv)
        for n in range(2):
            x = raw[n]
            for step in range(1, BEHIND + 1):
                place = BEHIND - step
                base = (BEHIND + 2 + place) * RUN
                before = last_rows(x, place)
                if step > 1:
                    before = jnp.where(step == my_index + 1, before, last_rows(x, BEHIND + 3 + place))
                x[base : base + PAD, :] = before
                x[base + PAD : base + RUN, :] = wrapped[step](n).astype(f32)
                first = (BEHIND + place) * HALF
                fields[n][first : first + HALF, :] = convolved(x, BEHIND + 2 + place, n + 1)

    for slot in range(SLOTS):
        source = pl.ds(pl.multiple_of(meta[slot] * BLK, BLK), BLK)
        for n in range(2):
            tables[n][slot * BLK : (slot + 1) * BLK, :] = fields[n][source, :]

    grads = cot[...]
    contract_last = (((1,), (1,)), ((), ()))
    contract_first = (((0,), (0,)), ((), ()))
    plain = (((1,), (0,)), ((), ()))
    chunk = 128
    chunks = [slice(c, c + chunk) for c in range(0, KEYS, chunk)]
    width = 2 * HALF

    def folded(x, op):
        return op(x.reshape(chunk // 8, 8, width), axis=0)

    factor = scale * math.log2(math.e)
    tops = None
    for c in chunks:
        s = lax.dot_general(kt[c, :], queries, contract_last, preferred_element_type=f32)
        s = s * factor + hide[c, :]
        scores[c, :] = s
        top = folded(s, jnp.max)
        tops = top if tops is None else jnp.maximum(tops, top)
    top = jnp.max(tops, axis=0, keepdims=True)
    totals = jnp.zeros((8, width), f32)
    for c in chunks:
        e = jnp.exp2(scores[c, :] - top)
        scores[c, :] = e
        totals = totals + folded(e, jnp.sum)
    inverse = 1.0 / jnp.sum(totals, axis=0, keepdims=True)
    deltas = jnp.zeros((8, width), f32)
    for c in chunks:
        p = scores[c, :] * inverse
        scores[c, :] = p
        pb = p.astype(half)
        probs_half[c, :] = pb
        dp = lax.dot_general(vt[c, :], grads, contract_last, preferred_element_type=f32)
        dprob[c, :] = dp
        deltas = deltas + folded(pb.astype(f32) * dp, jnp.sum)
    delta = jnp.sum(deltas, axis=0, keepdims=True)
    for number, c in enumerate(chunks):
        ds = (scores[c, :] * (dprob[c, :] - delta)).astype(half)
        dscore[c, :] = ds
        dk = lax.dot_general(ds, queries, plain, preferred_element_type=f32) * scale
        dv = lax.dot_general(probs_half[c, :], grads, plain, preferred_element_type=f32)
        for n, (out, term) in enumerate(((gk, dk), (gv, dv))):
            if c.start < SLOTS * BLK:
                for part in range(chunk // BLK):
                    slot = number * (chunk // BLK) + part
                    target = pl.ds(pl.multiple_of(meta[slot] * BLK, BLK), BLK)
                    out[target, :] = term[part * BLK : (part + 1) * BLK, :]
            else:
                first = c.start - SLOTS * BLK
                own_out[n, first : first + chunk, :] = term
    dq = lax.dot_general(dscore[...], kt[...], contract_first, preferred_element_type=f32) * scale
    dq_out[...] = dq

    def tap_sums(terms, x):
        sums = []
        for tap in range(TAPS):
            total = jnp.zeros((8, HEAD), f32)
            for rows, place in terms:
                base = place * RUN + PAD - tap
                total = total + jnp.sum((rows() * x[base : base + HALF, :]).reshape(HALF // 8, 8, HEAD), axis=0)
            sums.append(jnp.sum(total, axis=0, keepdims=True))
        return jnp.concatenate(sums, axis=0)

    taps_out[0] = tap_sums([(lambda s=s: dq_out[s * HALF : (s + 1) * HALF, :], s) for s in range(2)], xq)
    for n, g in enumerate((gk, gv)):
        terms = [(lambda p=p, g=g: g[p * HALF : (p + 1) * HALF, :], p) for p in range(BEHIND)]
        terms += [(lambda s=s, n=n: own_out[n, s * HALF : (s + 1) * HALF, :], BEHIND + s) for s in range(2)]
        taps_out[n + 1] = tap_sums(terms, raw[n])

    @pl.when(wrapping)
    def _():
        for n, g in enumerate((gk, gv)):
            terms = [
                (lambda p=p, g=g: g[(BEHIND + p) * HALF : (BEHIND + p + 1) * HALF, :], BEHIND + 2 + p)
                for p in range(BEHIND)
            ]
            taps_out[n + 1] = taps_out[n + 1] + tap_sums(terms, raw[n])

    for n, g in enumerate((gk, gv)):
        for step in range(1, BEHIND + 1):
            place = BEHIND - step
            low = g[place * HALF : (place + 1) * HALF, :]
            high = g[(BEHIND + place) * HALF : (BEHIND + place + 1) * HALF, :]
            if step % 2:
                odd_out[step // 2, n] = low.astype(half)
                e_odd_out[step // 2, n] = high.astype(half)
            else:
                even_out[step // 2 - 1, n] = low
                e_even_out[step // 2 - 1, n] = high


def attention_terms(group, heads, meta, key_pos, query_pos, tensors, weight, halos, near, wrapped):
    q_raw, k_raw, v_raw, cot = tensors
    first = group * heads
    smem = pl.BlockSpec(memory_space=pltpu.SMEM)

    def whole(shape):
        return pl.BlockSpec(shape, lambda h: (0,) * len(shape))

    def of_head(*lead):
        return pl.BlockSpec(lead + (HEAD,), lambda h: (0,) * len(lead) + (first + h,))

    def of_group(*lead):
        return pl.BlockSpec(lead + (HEAD,), lambda h: (0,) * len(lead) + (h,))

    rows = 2 * HALF
    channels = heads * HEAD
    f32 = jnp.float32
    half = jnp.bfloat16
    piece = of_group(2, HALF)
    pieces = of_group(3, 2, HALF)
    run = functools.partial(pltpu.VMEM)
    return pl.pallas_call(
        attention_kernel,
        grid=(heads,),
        in_specs=[
            smem, whole((KEYS, 1)), whole((1, rows)),
            of_head(rows), of_head(rows), of_head(rows), of_head(rows),
            of_head(3, TAPS), of_head(2, PAD), of_head(2, PAD), of_head(2, PAD),
            piece, piece, piece, pieces, piece, piece, piece, pieces,
        ],
        out_specs=[of_group(rows), of_group(2, rows), pieces, pieces, pieces, pieces, of_group(3, TAPS)],
        out_shape=[
            jax.ShapeDtypeStruct((rows, channels), f32),
            jax.ShapeDtypeStruct((2, rows, channels), f32),
            jax.ShapeDtypeStruct((3, 2, HALF, channels), half),
            jax.ShapeDtypeStruct((3, 2, HALF, channels), f32),
            jax.ShapeDtypeStruct((3, 2, HALF, channels), half),
            jax.ShapeDtypeStruct((3, 2, HALF, channels), f32),
            jax.ShapeDtypeStruct((3, TAPS, channels), f32),
        ],
        scratch_shapes=[
            run((KEYS, rows), f32),
            run((2 * RUN, HEAD), f32),
            run((14 * RUN, HEAD), f32), run((14 * RUN, HEAD), f32),
            run((2 * BEHIND * HALF, HEAD), half), run((2 * BEHIND * HALF, HEAD), half),
            run((KEYS, HEAD), half), run((KEYS, HEAD), half),
            run((KEYS, rows), f32), run((KEYS, rows), f32),
            run((KEYS, rows), half), run((KEYS, rows), half),
            run((2 * BEHIND * HALF, HEAD), f32), run((2 * BEHIND * HALF, HEAD), f32),
        ],
        compiler_params=pltpu.CompilerParams(vmem_limit_bytes=VMEM),
        cost_estimate=pl.CostEstimate(
            flops=heads * 10 * rows * KEYS * HEAD, bytes_accessed=heads * 3 * 1024 * 1024, transcendentals=heads * rows * KEYS
        ),
        name="attention",
    )(meta, key_pos, query_pos, q_raw, k_raw, v_raw, cot, weight, *halos, *near, *wrapped)


def unconvolved(rows, after, taps):
    extended = jnp.concatenate([rows, after], axis=0)
    total = taps[0:1, :] * extended[:HALF, :]
    for tap in range(1, TAPS):
        total = total + taps[tap : tap + 1, :] * extended[tap : tap + HALF, :]
    return total.astype(jnp.bfloat16)


def query_kernel(grad, after, weight, out):
    for side in range(2):
        rows = slice(side * HALF, (side + 1) * HALF)
        out[rows, :] = unconvolved(grad[rows, :], after[side], weight[0])


def final_kernel(meta, own, two, four, six, beside, e_two, e_four, e_six, after, weight, *rest):
    outs = rest[-2:]
    f32 = jnp.float32
    first_core = meta[0] % 2 == 0
    for n in range(2):
        low = own[n, 0:HALF, :] + two[n].astype(f32) + four[n].astype(f32) + six[n].astype(f32)
        low = low + jnp.where(first_core, beside[0, n].astype(f32), 0.0)
        high = own[n, HALF : 2 * HALF, :] + e_two[n].astype(f32) + e_four[n].astype(f32) + e_six[n].astype(f32)
        outs[n][0:HALF, :] = unconvolved(low, after[n, 0], weight[n + 1])
        outs[n][HALF : 2 * HALF, :] = unconvolved(high, after[n, 1], weight[n + 1])


def finished(group, heads, meta, own, near, beside, wrapped, after, weight, earlier):
    rows = 2 * HALF
    channels = heads * HEAD
    first = group * heads

    def of_group(*lead):
        return pl.BlockSpec(lead + (HEAD,), lambda h: (0,) * len(lead) + (h,))

    def of_head(*lead):
        return pl.BlockSpec(lead + (HEAD,), lambda h: (0,) * len(lead) + (first + h,))

    piece = of_group(2, HALF)
    anywhere = pl.BlockSpec(memory_space=pl.ANY)
    shape = jax.ShapeDtypeStruct((rows, GROUPS * channels), jnp.bfloat16)
    extra = [] if earlier is None else list(earlier)
    return pl.pallas_call(
        final_kernel,
        grid=(heads,),
        in_specs=[
            pl.BlockSpec(memory_space=pltpu.SMEM), of_group(2, rows), piece, piece, piece,
            of_group(1, 2, HALF), piece, piece, piece, of_group(2, 2, PAD), of_head(3, TAPS),
        ]
        + [anywhere] * len(extra),
        out_specs=[of_head(rows), of_head(rows)],
        out_shape=[shape, shape],
        input_output_aliases={11 + n: n for n in range(len(extra))},
        compiler_params=pltpu.CompilerParams(vmem_limit_bytes=VMEM),
        name="finish",
    )(meta, own, *near, beside, *wrapped, after, weight, *extra)


def body(query_in, key_in, value_in, conv_weight, out_grad, block_lists):
    q_raw, k_raw, v_raw, cot = (x[0] for x in (query_in, key_in, value_in, out_grad))
    f32 = jnp.float32
    half = jnp.bfloat16
    channels = q_raw.shape[1]
    rows = 2 * HALF
    heads = channels // HEAD // GROUPS
    width = heads * HEAD
    count = lax.axis_size("ctx")
    my_index = lax.axis_index("ctx")
    first_core = my_index % 2 == 0
    is_last = my_index == count - 1
    up = [(i, i + 1) for i in range(count - 1)]
    down = [(i + 1, i) for i in range(count - 1)]
    every = sibling_pairs(count)
    few = sibling_pairs(BEHIND)

    near = []
    wrapped = []
    for group in range(GROUPS):
        part = slice(group * width, (group + 1) * width)
        low = jnp.stack([k_raw[:HALF, part], v_raw[:HALF, part]])
        high = jnp.stack([k_raw[HALF:, part], v_raw[HALF:, part]])
        two = along(low, ring_pairs(count, 2))
        six = along(low, ring_pairs(count, 6))
        if group == 0:
            four = along(low, ring_pairs(count, 4))
        else:
            four = along(six, ring_pairs(count, -2))
        e_two = along(high, wrapped_out(count, 2))
        e_six = along(high, wrapped_out(count, 6))
        e_four = along(e_six, [(i + 2, i) for i in range(4)])
        near.append((two, four, six, shared(low, two, four, six, first_core, every)))
        wrapped.append((e_two, e_four, e_six, shared(high, e_two, e_four, e_six, first_core, few)))

    tail = slice(HALF - PAD, HALF)
    high_tail = slice(rows - PAD, rows)
    q_before = along(q_raw[tail], up)
    far = along(jnp.stack([k_raw[tail], v_raw[tail]]), ring_pairs(count, BEHIND + 1))
    above = along(jnp.stack([x[high_tail] for x in (q_raw, k_raw, v_raw)]), down)
    below = jnp.stack([x[tail] for x in (q_raw, k_raw, v_raw)])
    above = jnp.where(is_last, below, above).astype(f32)
    q_halo = jnp.stack([q_before.astype(f32), above[0]])
    halos = (q_halo, far.astype(f32), above[1:])

    index, remote_pos = table_of_slots(block_lists[0], my_index, count)
    spread = jnp.arange(HALF, dtype=jnp.int32)
    positions = jnp.concatenate([my_index * HALF + spread, (2 * count - 1 - my_index) * HALF + spread])
    key_pos = jnp.concatenate([remote_pos, positions])[:, None]
    place = my_index[None].astype(jnp.int32)
    meta = jnp.concatenate([index, place]).astype(jnp.int32)

    results = [
        attention_terms(
            group, heads, meta, key_pos, positions[None, :], (q_raw, k_raw, v_raw, cot), conv_weight, halos,
            near[group], wrapped[group],
        )
        for group in range(GROUPS)
    ]

    returned = []
    for dq, own, odd, even, e_odd, e_even, taps in results:
        sides = []
        for odds, evens, pairs, back in (
            (odd, even, every, lambda by: ring_pairs(count, -by)),
            (e_odd, e_even, few, lambda by: wrapped_back(count, by)),
        ):
            got = along(odds, pairs)
            wide = got.astype(f32)
            sums = [
                evens[0] + jnp.where(first_core, wide[1], wide[0]),
                evens[1] + jnp.where(first_core, wide[2], wide[1]),
                evens[2] + jnp.where(first_core, 0.0, wide[2]),
            ]
            sent = [along(total.astype(half), back(2 * n + 2)) for n, total in enumerate(sums)]
            sides.append((sent, got))
        returned.append(sides)

    kernel_terms = jnp.concatenate([r[6] for r in results], axis=2)
    kernel_grad = summed_over(summed_over(kernel_terms, "ctx"), "dp")

    def after_rows(heads_of):
        low, high = heads_of
        next_low = along(low, down)
        next_high = along(high, up)
        return jnp.stack([jnp.where(is_last, high, next_low), next_high], axis=-3)

    dq = jnp.concatenate([r[0] for r in results], axis=1)
    q_after = after_rows((dq[:PAD], dq[HALF : HALF + PAD]))
    spec = pl.BlockSpec((rows, HEAD), lambda h: (0, h))
    query_grad = pl.pallas_call(
        query_kernel,
        grid=(channels // HEAD,),
        in_specs=[
            spec,
            pl.BlockSpec((2, PAD, HEAD), lambda h: (0, 0, h)),
            pl.BlockSpec((3, TAPS, HEAD), lambda h: (0, 0, h)),
        ],
        out_specs=spec,
        out_shape=jax.ShapeDtypeStruct((rows, channels), half),
        compiler_params=pltpu.CompilerParams(vmem_limit_bytes=VMEM),
        name="query_finish",
    )(dq, q_after, conv_weight)

    outs = None
    for group in range(GROUPS):
        own = results[group][1]
        (sent, got), (e_sent, _) = returned[group]
        low = own[:, :PAD] + jnp.where(first_core, got[0, :, :PAD].astype(f32), 0.0)
        high = own[:, HALF : HALF + PAD]
        for n in range(3):
            low = low + sent[n][:, :PAD].astype(f32)
            high = high + e_sent[n][:, :PAD].astype(f32)
        after = after_rows((low, high))
        outs = finished(group, heads, place, own, sent, got, e_sent, after, conv_weight, outs)
    return (query_grad[None], outs[0][None], outs[1][None], kernel_grad)


def solution(mesh):
    placed = (
        P("dp", "ctx", None),
        P("dp", "ctx", None),
        P("dp", "ctx", None),
        P(),
        P("dp", "ctx", None),
        P("dp", "ctx", None),
    )
    return jax.shard_map(
        body,
        mesh=mesh,
        in_specs=placed,
        out_specs=(P("dp", "ctx", None), P("dp", "ctx", None), P("dp", "ctx", None), P()),
        check_vma=False,
    )
```

```python
import functools
import math

import jax
import jax.numpy as jnp
from jax import lax
from jax.experimental import pallas as pl
from jax.experimental.pallas import tpu as pltpu
from jax.sharding import PartitionSpec as P

HEAD = 128
TAPS = 4
BLK = 64
BEHIND = 6
MAX_REMOTE = 2
HALF = 128
OWN_BLOCKS = 4
PAD = 8
RUN = HALF + PAD
SLOTS = BEHIND * MAX_REMOTE
KEYS = SLOTS * BLK + 2 * HALF
GROUPS = 2
HIDDEN = 1 << 30
WIDE = 512
VMEM = 48 * 1024 * 1024


def along(x, pairs):
    return lax.ppermute(x, "ctx", pairs)


def ring_pairs(count, by):
    return [(i, (i + by) % count) for i in range(count)]


def sibling_pairs(count):
    return [(i, i ^ 1) for i in range(count)]


def wrapped_out(count, by):
    return [(i, i + by - count) for i in range(count - by, count)]


def wrapped_back(count, by):
    return [(j, i) for i, j in wrapped_out(count, by)]


def once(x, *others):
    return lax.optimization_barrier((x, others))[0]


def summed_over(x, axes, after):
    number = 0
    for axis in axes:
        count = lax.axis_size(axis)
        step = 1
        while step < count:
            x = once(x, *after.get(number, ()))
            x = x + lax.ppermute(x, axis, [(i, i ^ step) for i in range(count)])
            step *= 2
            number += 1
    return x


def shared(own, from_two, from_four, from_six, first_core, pairs):
    mine = jnp.stack(
        [
            jnp.where(first_core, own, from_two),
            jnp.where(first_core, from_two, from_four),
            jnp.where(first_core, from_four, from_six),
        ]
    )
    return along(mine, pairs)


def table_of_slots(lists, my_index, count):
    span = lists * BLK // HALF
    upper = span >= count
    owners = jnp.where(upper, 2 * count - 1 - span, span)
    local = jnp.where(upper, OWN_BLOCKS // 2, 0) + lists % (HALF // BLK)
    distance = ((my_index - owners) % count).reshape(-1)
    reach = BEHIND - jnp.arange(BEHIND, dtype=jnp.int32)
    block_ids = jnp.arange(OWN_BLOCKS, dtype=jnp.int32)
    wanted = jnp.any(
        (distance[:, None, None] == reach[None, :, None])
        & (local.reshape(-1)[:, None, None] == block_ids[None, None, :]),
        axis=0,
    )
    rank = jnp.cumsum(wanted.astype(jnp.int32), axis=1) - 1
    slot_ids = jnp.arange(MAX_REMOTE, dtype=jnp.int32)
    hits = wanted[:, :, None] & (rank[:, :, None] == slot_ids[None, None, :])
    chosen = jnp.sum(jnp.where(hits, block_ids[None, :, None], 0), axis=1)
    chosen_named = jnp.any(hits, axis=1)
    wraps = (reach > my_index)[:, None]
    block = jnp.where(wraps, chosen, slot_ids[None, :])
    named = jnp.where(wraps, chosen_named, wanted[:, :MAX_REMOTE])
    rows = jnp.arange(BEHIND, dtype=jnp.int32)[:, None]
    index = jnp.where(block < 2, rows * 2 + block, SLOTS + rows * 2 + block - 2)
    owner = ((my_index - reach) % count)[:, None]
    piece = jnp.where(block < 2, owner, 2 * count - 1 - owner)
    start = piece * HALF + (block % 2) * BLK
    start = jnp.where(named, start, HIDDEN)
    spread = jnp.arange(BLK, dtype=jnp.int32)
    positions = (start.reshape(-1)[:, None] + spread[None, :]).reshape(-1)
    return index.reshape(-1), positions


def attention_kernel(
    meta, key_pos, query_pos, q_raw, k_raw, v_raw, cot, weight, q_halo, far_halo, high_halo,
    two, four, six, odd, e_two, e_four, e_six, e_odd,
    dq_out, own_out, odd_out, even_out, e_odd_out, e_even_out, taps_out,
    hide, xq, xk, xv, kall, vall, kt, vt, scores, dprob, probs_half, dscore, gk, gv,
):
    my_index = meta[SLOTS]
    wrapping = my_index < BEHIND
    scale = HEAD ** -0.5
    f32 = jnp.float32
    half = jnp.bfloat16

    @pl.when(pl.program_id(0) == 0)
    def _():
        hide[...] = jnp.where(key_pos[...] <= query_pos[...], 0.0, -jnp.inf)
        gk[...] = jnp.zeros_like(gk)
        gv[...] = jnp.zeros_like(gv)

    raw = (xk, xv)
    fields = (kall, vall)
    tables = (kt, vt)
    near = {1: lambda n: odd[0, n], 3: lambda n: odd[1, n], 5: lambda n: odd[2, n],
            2: lambda n: two[n], 4: lambda n: four[n], 6: lambda n: six[n]}
    wrapped = {1: lambda n: e_odd[0, n], 3: lambda n: e_odd[1, n], 5: lambda n: e_odd[2, n],
               2: lambda n: e_two[n], 4: lambda n: e_four[n], 6: lambda n: e_six[n]}

    def convolved(x, place, which):
        base = place * RUN + PAD
        total = weight[which, 0:1, :] * x[base : base + HALF, :]
        for tap in range(1, TAPS):
            total = total + weight[which, tap : tap + 1, :] * x[base - tap : base - tap + HALF, :]
        return total.astype(half)

    def last_rows(x, place):
        return x[place * RUN + HALF : place * RUN + RUN, :]

    for side in range(2):
        xq[side * RUN : side * RUN + PAD, :] = q_halo[side]
        xq[side * RUN + PAD : (side + 1) * RUN, :] = q_raw[side * HALF : (side + 1) * HALF, :].astype(f32)
    queries = jnp.concatenate([convolved(xq, 0, 0), convolved(xq, 1, 0)], axis=0)

    own_raw = (k_raw, v_raw)
    for n in range(2):
        x = raw[n]
        for place in range(BEHIND + 1):
            base = place * RUN
            if place < BEHIND:
                rows = near[BEHIND - place](n).astype(f32)
            else:
                rows = own_raw[n][0:HALF, :].astype(f32)
            before = far_halo[n] if place == 0 else last_rows(x, place - 1)
            x[base : base + PAD, :] = jnp.where(BEHIND - place == my_index, 0.0, before)
            x[base + PAD : base + RUN, :] = rows
        base = (BEHIND + 1) * RUN
        x[base : base + PAD, :] = high_halo[n]
        x[base + PAD : base + RUN, :] = own_raw[n][HALF : 2 * HALF, :].astype(f32)
        for place in range(BEHIND):
            fields[n][place * HALF : (place + 1) * HALF, :] = convolved(x, place, n + 1)
        for side in range(2):
            first = SLOTS * BLK + side * HALF
            tables[n][first : first + HALF, :] = convolved(x, BEHIND + side, n + 1)

    @pl.when(wrapping)
    def _():
        gk[...] = jnp.zeros_like(gk)
        gv[...] = jnp.zeros_like(gv)
        for n in range(2):
            x = raw[n]
            for step in range(1, BEHIND + 1):
                place = BEHIND - step
                base = (BEHIND + 2 + place) * RUN
                before = last_rows(x, place)
                if step > 1:
                    before = jnp.where(step == my_index + 1, before, last_rows(x, BEHIND + 3 + place))
                x[base : base + PAD, :] = before
                x[base + PAD : base + RUN, :] = wrapped[step](n).astype(f32)
                first = (BEHIND + place) * HALF
                fields[n][first : first + HALF, :] = convolved(x, BEHIND + 2 + place, n + 1)

    for slot in range(SLOTS):
        source = pl.ds(pl.multiple_of(meta[slot] * BLK, BLK), BLK)
        for n in range(2):
            tables[n][slot * BLK : (slot + 1) * BLK, :] = fields[n][source, :]

    grads = cot[...]
    contract_last = (((1,), (1,)), ((), ()))
    contract_first = (((0,), (0,)), ((), ()))
    plain = (((1,), (0,)), ((), ()))
    chunk = 128
    chunks = [slice(c, c + chunk) for c in range(0, KEYS, chunk)]
    width = 2 * HALF

    def folded(x, op):
        return op(x.reshape(chunk // 8, 8, width), axis=0)

    factor = scale * math.log2(math.e)
    tops = None
    for c in chunks:
        s = lax.dot_general(kt[c, :], queries, contract_last, preferred_element_type=f32)
        s = s * factor + hide[c, :]
        scores[c, :] = s
        top = folded(s, jnp.max)
        tops = top if tops is None else jnp.maximum(tops, top)
    top = jnp.max(tops, axis=0, keepdims=True)
    totals = jnp.zeros((8, width), f32)
    for c in chunks:
        e = jnp.exp2(scores[c, :] - top)
        scores[c, :] = e
        totals = totals + folded(e, jnp.sum)
    inverse = 1.0 / jnp.sum(totals, axis=0, keepdims=True)
    deltas = jnp.zeros((8, width), f32)
    for c in chunks:
        p = scores[c, :] * inverse
        scores[c, :] = p
        pb = p.astype(half)
        probs_half[c, :] = pb
        dp = lax.dot_general(vt[c, :], grads, contract_last, preferred_element_type=f32)
        dprob[c, :] = dp
        deltas = deltas + folded(pb.astype(f32) * dp, jnp.sum)
    delta = jnp.sum(deltas, axis=0, keepdims=True)
    for number, c in enumerate(chunks):
        ds = (scores[c, :] * (dprob[c, :] - delta)).astype(half)
        dscore[c, :] = ds
        dk = lax.dot_general(ds, queries, plain, preferred_element_type=f32) * scale
        dv = lax.dot_general(probs_half[c, :], grads, plain, preferred_element_type=f32)
        for n, (out, term) in enumerate(((gk, dk), (gv, dv))):
            if c.start < SLOTS * BLK:
                for part in range(chunk // BLK):
                    slot = number * (chunk // BLK) + part
                    target = pl.ds(pl.multiple_of(meta[slot] * BLK, BLK), BLK)
                    out[target, :] = term[part * BLK : (part + 1) * BLK, :]
            else:
                first = c.start - SLOTS * BLK
                own_out[n, first : first + chunk, :] = term
    dq = lax.dot_general(dscore[...], kt[...], contract_first, preferred_element_type=f32) * scale
    dq_out[...] = dq

    def tap_sums(terms, x):
        sums = []
        for tap in range(TAPS):
            total = jnp.zeros((8, HEAD), f32)
            for rows, place in terms:
                base = place * RUN + PAD - tap
                total = total + jnp.sum((rows() * x[base : base + HALF, :]).reshape(HALF // 8, 8, HEAD), axis=0)
            sums.append(jnp.sum(total, axis=0, keepdims=True))
        return jnp.concatenate(sums, axis=0)

    taps_out[0] = tap_sums([(lambda s=s: dq_out[s * HALF : (s + 1) * HALF, :], s) for s in range(2)], xq)
    for n, g in enumerate((gk, gv)):
        terms = [(lambda p=p, g=g: g[p * HALF : (p + 1) * HALF, :], p) for p in range(BEHIND)]
        terms += [(lambda s=s, n=n: own_out[n, s * HALF : (s + 1) * HALF, :], BEHIND + s) for s in range(2)]
        taps_out[n + 1] = tap_sums(terms, raw[n])

    @pl.when(wrapping)
    def _():
        for n, g in enumerate((gk, gv)):
            terms = [
                (lambda p=p, g=g: g[(BEHIND + p) * HALF : (BEHIND + p + 1) * HALF, :], BEHIND + 2 + p)
                for p in range(BEHIND)
            ]
            taps_out[n + 1] = taps_out[n + 1] + tap_sums(terms, raw[n])

    for n, g in enumerate((gk, gv)):
        for step in range(1, BEHIND + 1):
            place = BEHIND - step
            low = g[place * HALF : (place + 1) * HALF, :]
            high = g[(BEHIND + place) * HALF : (BEHIND + place + 1) * HALF, :]
            if step % 2:
                odd_out[step // 2, n] = low.astype(half)
                e_odd_out[step // 2, n] = high.astype(half)
            else:
                even_out[step // 2 - 1, n] = low
                e_even_out[step // 2 - 1, n] = high


def attention_terms(group, heads, meta, key_pos, query_pos, tensors, weight, halos, near, wrapped):
    q_raw, k_raw, v_raw, cot = tensors
    first = group * heads
    smem = pl.BlockSpec(memory_space=pltpu.SMEM)

    def whole(shape):
        return pl.BlockSpec(shape, lambda h: (0,) * len(shape))

    def of_head(*lead):
        return pl.BlockSpec(lead + (HEAD,), lambda h: (0,) * len(lead) + (first + h,))

    def of_group(*lead):
        return pl.BlockSpec(lead + (HEAD,), lambda h: (0,) * len(lead) + (h,))

    rows = 2 * HALF
    channels = heads * HEAD
    f32 = jnp.float32
    half = jnp.bfloat16
    piece = of_group(2, HALF)
    pieces = of_group(3, 2, HALF)
    run = functools.partial(pltpu.VMEM)
    return pl.pallas_call(
        attention_kernel,
        grid=(heads,),
        in_specs=[
            smem, whole((KEYS, 1)), whole((1, rows)),
            of_head(rows), of_head(rows), of_head(rows), of_head(rows),
            of_head(3, TAPS), of_head(2, PAD), of_head(2, PAD), of_head(2, PAD),
            piece, piece, piece, pieces, piece, piece, piece, pieces,
        ],
        out_specs=[of_group(rows), of_group(2, rows), pieces, pieces, pieces, pieces, of_group(3, TAPS)],
        out_shape=[
            jax.ShapeDtypeStruct((rows, channels), f32),
            jax.ShapeDtypeStruct((2, rows, channels), f32),
            jax.ShapeDtypeStruct((3, 2, HALF, channels), half),
            jax.ShapeDtypeStruct((3, 2, HALF, channels), f32),
            jax.ShapeDtypeStruct((3, 2, HALF, channels), half),
            jax.ShapeDtypeStruct((3, 2, HALF, channels), f32),
            jax.ShapeDtypeStruct((3, TAPS, channels), f32),
        ],
        scratch_shapes=[
            run((KEYS, rows), f32),
            run((2 * RUN, HEAD), f32),
            run((14 * RUN, HEAD), f32), run((14 * RUN, HEAD), f32),
            run((2 * BEHIND * HALF, HEAD), half), run((2 * BEHIND * HALF, HEAD), half),
            run((KEYS, HEAD), half), run((KEYS, HEAD), half),
            run((KEYS, rows), f32), run((KEYS, rows), f32),
            run((KEYS, rows), half), run((KEYS, rows), half),
            run((2 * BEHIND * HALF, HEAD), f32), run((2 * BEHIND * HALF, HEAD), f32),
        ],
        compiler_params=pltpu.CompilerParams(vmem_limit_bytes=VMEM),
        cost_estimate=pl.CostEstimate(
            flops=heads * 100 * rows * KEYS * HEAD, bytes_accessed=heads * 3 * 1024 * 1024, transcendentals=heads * rows * KEYS
        ),
        name="attention",
    )(meta, key_pos, query_pos, q_raw, k_raw, v_raw, cot, weight, *halos, *near, *wrapped)


def unconvolved(rows, after, taps):
    extended = jnp.concatenate([rows, after], axis=0)
    total = taps[0:1, :] * extended[:HALF, :]
    for tap in range(1, TAPS):
        total = total + taps[tap : tap + 1, :] * extended[tap : tap + HALF, :]
    return total.astype(jnp.bfloat16)


def query_kernel(grad, after, weight, out):
    for side in range(2):
        rows = slice(side * HALF, (side + 1) * HALF)
        out[rows, :] = unconvolved(grad[rows, :], after[side], weight[0])


def final_kernel(terms, meta, own, beside, after, weight, *rest):
    outs = rest[-2:]
    sent = rest[:terms]
    e_sent = rest[terms : terms + 2]
    f32 = jnp.float32
    first_core = meta[0] % 2 == 0
    for n in range(2):
        low = own[n, 0:HALF, :] + jnp.where(first_core, beside[0, n].astype(f32), 0.0)
        for x in sent:
            low = low + x[n].astype(f32)
        high = own[n, HALF : 2 * HALF, :]
        for x in e_sent:
            high = high + x[n].astype(f32)
        outs[n][0:HALF, :] = unconvolved(low, after[n, 0], weight[n + 1])
        outs[n][HALF : 2 * HALF, :] = unconvolved(high, after[n, 1], weight[n + 1])


def combine_kernel(meta, even, odd, e_even, e_odd, two, four, six, e_two, e_four, e_six):
    f32 = jnp.float32
    first_core = meta[0] % 2 == 0
    for evens, odds, outs in ((even, odd, (two, four, six)), (e_even, e_odd, (e_two, e_four, e_six))):
        for n in range(2):
            wide = [odds[m, n].astype(f32) for m in range(3)]
            beside = [
                jnp.where(first_core, wide[1], wide[0]),
                jnp.where(first_core, wide[2], wide[1]),
                jnp.where(first_core, 0.0, wide[2]),
            ]
            for m, out in enumerate(outs):
                out[n] = (evens[m, n] + beside[m]).astype(out.dtype)


def combined(meta, even, odd, e_even, e_odd, six_type):
    channels = even.shape[-1]
    wide = min(WIDE, channels)
    half = jnp.bfloat16
    f32 = jnp.float32
    pieces = pl.BlockSpec((3, 2, HALF, wide), lambda h: (0, 0, 0, h))
    piece = pl.BlockSpec((2, HALF, wide), lambda h: (0, 0, h))
    types = [half, half, six_type, half, half, f32]
    return pl.pallas_call(
        combine_kernel,
        grid=(channels // wide,),
        in_specs=[pl.BlockSpec(memory_space=pltpu.SMEM)] + [pieces] * 4,
        out_specs=[piece] * 6,
        out_shape=[jax.ShapeDtypeStruct((2, HALF, channels), t) for t in types],
        compiler_params=pltpu.CompilerParams(vmem_limit_bytes=VMEM),
        name="combine",
    )(meta, even, odd, e_even, e_odd)


def finished(group, heads, meta, own, near, beside, wrapped, after, weight, earlier):
    rows = 2 * HALF
    channels = heads * HEAD
    wide = min(WIDE, channels)
    first = group * (channels // wide)

    def of_group(*lead):
        return pl.BlockSpec(lead + (wide,), lambda h: (0,) * len(lead) + (h,))

    def of_head(*lead):
        return pl.BlockSpec(lead + (wide,), lambda h: (0,) * len(lead) + (first + h,))

    piece = of_group(2, HALF)
    anywhere = pl.BlockSpec(memory_space=pl.ANY)
    shape = jax.ShapeDtypeStruct((rows, GROUPS * channels), jnp.bfloat16)
    extra = [] if earlier is None else list(earlier)
    terms = len(near) + len(wrapped)
    return pl.pallas_call(
        functools.partial(final_kernel, len(near)),
        grid=(channels // wide,),
        in_specs=[
            pl.BlockSpec(memory_space=pltpu.SMEM), of_group(2, rows), of_group(1, 2, HALF),
            of_head(2, 2, PAD), of_head(3, TAPS),
        ]
        + [piece] * terms
        + [anywhere] * len(extra),
        out_specs=[of_head(rows), of_head(rows)],
        out_shape=[shape, shape],
        input_output_aliases={5 + terms + n: n for n in range(len(extra))},
        compiler_params=pltpu.CompilerParams(vmem_limit_bytes=VMEM),
        name="finish",
    )(meta, own, beside, after, weight, *near, *wrapped, *extra)


def body(query_in, key_in, value_in, conv_weight, out_grad, block_lists):
    q_raw, k_raw, v_raw, cot = (x[0] for x in (query_in, key_in, value_in, out_grad))
    f32 = jnp.float32
    half = jnp.bfloat16
    channels = q_raw.shape[1]
    rows = 2 * HALF
    heads = channels // HEAD // GROUPS
    width = heads * HEAD
    count = lax.axis_size("ctx")
    my_index = lax.axis_index("ctx")
    first_core = my_index % 2 == 0
    is_last = my_index == count - 1
    up = [(i, i + 1) for i in range(count - 1)]
    down = [(i + 1, i) for i in range(count - 1)]
    every = sibling_pairs(count)
    few = sibling_pairs(BEHIND)

    tail = slice(HALF - PAD, HALF)
    high_tail = slice(rows - PAD, rows)
    q_before = along(q_raw[tail], up)
    far = along(jnp.stack([k_raw[tail], v_raw[tail]]), ring_pairs(count, BEHIND + 1))
    above = along(jnp.stack([x[high_tail] for x in (q_raw, k_raw, v_raw)]), down)

    near = []
    wrapped = []
    for group in range(GROUPS):
        part = slice(group * width, (group + 1) * width)
        low = jnp.stack([k_raw[:HALF, part], v_raw[:HALF, part]])
        high = jnp.stack([k_raw[HALF:, part], v_raw[HALF:, part]])
        if group:
            low, high = once((low, high), ready)
        two = along(low, ring_pairs(count, 2))
        six = along(low, ring_pairs(count, 6))
        if group == 0:
            ready = once(six, q_before, far, above)
            four = along(ready, ring_pairs(count, -2))
        else:
            four = along(low, ring_pairs(count, 4))
        e_two = along(high, wrapped_out(count, 2))
        e_six = along(high, wrapped_out(count, 6))
        e_four = along(e_six, [(i + 2, i) for i in range(4)])
        near.append((two, four, six, low))
        wrapped.append((e_two, e_four, e_six, high))

    below = jnp.stack([x[tail] for x in (q_raw, k_raw, v_raw)])
    above = jnp.where(is_last, below, above).astype(f32)
    q_halo = jnp.stack([q_before.astype(f32), above[0]])
    halos = (q_halo, far.astype(f32), above[1:])

    index, remote_pos = table_of_slots(block_lists[0], my_index, count)
    spread = jnp.arange(HALF, dtype=jnp.int32)
    positions = jnp.concatenate([my_index * HALF + spread, (2 * count - 1 - my_index) * HALF + spread])
    key_pos = jnp.concatenate([remote_pos, positions])[:, None]
    place = my_index[None].astype(jnp.int32)
    meta = jnp.concatenate([index, place]).astype(jnp.int32)

    results = []
    returned = []
    for group in range(GROUPS):
        two, four, six, low = near[group]
        e_two, e_four, e_six, high = wrapped[group]
        if group:
            low, high = once((low, high), results[-1][6])
        else:
            low, high = once((low, high), near[1][0])
        beside = shared(low, two, four, six, first_core, every)
        e_beside = shared(high, e_two, e_four, e_six, first_core, few)
        result = attention_terms(
            group, heads, meta, key_pos, positions[None, :], (q_raw, k_raw, v_raw, cot), conv_weight, halos,
            (two, four, six, beside), (e_two, e_four, e_six, e_beside),
        )
        _, _, odd, even, e_odd, e_even, _ = result
        if group:
            odd, e_odd = once((odd, e_odd), *returned[-1][0], returned[-1][2][0], e_merged)
        got = along(odd, every)
        e_got = along(e_odd, few)
        direct = group == 0
        two, four, six, e_two, e_four, e_six = combined(place, even, got, e_even, e_got, half if direct else f32)
        meta = once(meta, two)
        sent_two = along(two, ring_pairs(count, -2))
        if direct:
            sent_four = along(four, ring_pairs(count, -4))
        else:
            six = (six + along(four, ring_pairs(count, 2)).astype(f32)).astype(half)
        sent_six = along(six, ring_pairs(count, -6))
        e_sent_two = along(e_two, wrapped_back(count, 2))
        e_six = (e_six + along(e_four, [(i, i + 2) for i in range(4)]).astype(f32)).astype(half)
        e_merged = e_six
        e_sent_six = along(e_six, wrapped_back(count, 6))
        sent = (sent_two, sent_four, sent_six) if direct else (sent_two, sent_six)
        results.append(result)
        returned.append((sent, got, (e_sent_two, e_sent_six)))
        last_two = two

    kernel_terms = jnp.concatenate([r[6] for r in results], axis=2)
    first_sent = (returned[-1][0][0], returned[-1][2][0])
    kernel_grad = summed_over(kernel_terms, ("ctx", "dp"), {2: (last_two,), 4: first_sent})

    def after_rows(heads_of):
        low, high = heads_of
        next_low = along(low, down)
        next_high = along(high, up)
        return jnp.stack([jnp.where(is_last, high, next_low), next_high], axis=-3)

    dq = once(jnp.concatenate([r[0] for r in results], axis=1), *first_sent)
    q_after = after_rows((dq[:PAD], dq[HALF : HALF + PAD]))
    wide = min(WIDE, width)
    spec = pl.BlockSpec((rows, wide), lambda h: (0, h))
    query_grad = pl.pallas_call(
        query_kernel,
        grid=(channels // wide,),
        in_specs=[
            spec,
            pl.BlockSpec((2, PAD, wide), lambda h: (0, 0, h)),
            pl.BlockSpec((3, TAPS, wide), lambda h: (0, 0, h)),
        ],
        out_specs=spec,
        out_shape=jax.ShapeDtypeStruct((rows, channels), half),
        compiler_params=pltpu.CompilerParams(vmem_limit_bytes=VMEM),
        name="query_finish",
    )(dq, q_after, conv_weight)

    lows = []
    highs = []
    for group in range(GROUPS):
        own = results[group][1]
        sent, got, e_sent = returned[group]
        low = own[:, :PAD] + jnp.where(first_core, got[0, :, :PAD].astype(f32), 0.0)
        high = own[:, HALF : HALF + PAD]
        for x in sent:
            low = low + x[:, :PAD].astype(f32)
        for x in e_sent:
            high = high + x[:, :PAD].astype(f32)
        lows.append(low)
        highs.append(high)
    after = after_rows((jnp.concatenate(lows, axis=2), jnp.concatenate(highs, axis=2)))
    outs = None
    for group in range(GROUPS):
        sent, got, e_sent = returned[group]
        outs = finished(group, heads, place, results[group][1], sent, got, e_sent, after, conv_weight, outs)
    return (query_grad[None], outs[0][None], outs[1][None], kernel_grad)


def solution(mesh):
    placed = (
        P("dp", "ctx", None),
        P("dp", "ctx", None),
        P("dp", "ctx", None),
        P(),
        P("dp", "ctx", None),
        P("dp", "ctx", None),
    )
    return jax.shard_map(
        body,
        mesh=mesh,
        in_specs=placed,
        out_specs=(P("dp", "ctx", None), P("dp", "ctx", None), P("dp", "ctx", None), P()),
        check_vma=False,
    )
```

```python
import functools
import math

import jax
import jax.numpy as jnp
from jax import lax
from jax.experimental import pallas as pl
from jax.experimental.pallas import tpu as pltpu
from jax.sharding import PartitionSpec as P

HEAD = 128
TAPS = 4
BLK = 64
BEHIND = 6
MAX_REMOTE = 2
HALF = 128
OWN_BLOCKS = 4
PAD = 8
RUN = HALF + PAD
SLOTS = BEHIND * MAX_REMOTE
KEYS = SLOTS * BLK + 2 * HALF
GROUPS = 2
HIDDEN = 1 << 30
WIDE = 512
VMEM = 48 * 1024 * 1024


def along(x, pairs):
    return lax.ppermute(x, "ctx", pairs)


def ring_pairs(count, by):
    return [(i, (i + by) % count) for i in range(count)]


def sibling_pairs(count):
    return [(i, i ^ 1) for i in range(count)]


def wrapped_out(count, by):
    return [(i, i + by - count) for i in range(count - by, count)]


def wrapped_back(count, by):
    return [(j, i) for i, j in wrapped_out(count, by)]


def once(x, *others):
    return lax.optimization_barrier((x, others))[0]


def exchange_steps(axes):
    steps = []
    for axis in axes:
        step = 1
        while step < lax.axis_size(axis):
            steps.append((axis, step))
            step *= 2
    return steps


def exchanged(x, steps):
    for axis, step in steps:
        x = x + lax.ppermute(x, axis, [(i, i ^ step) for i in range(lax.axis_size(axis))])
    return x


def shared(own, from_two, from_four, from_six, first_core, pairs):
    mine = jnp.stack(
        [
            jnp.where(first_core, own, from_two),
            jnp.where(first_core, from_two, from_four),
            jnp.where(first_core, from_four, from_six),
        ]
    )
    return along(mine, pairs)


def table_of_slots(lists, my_index, count):
    span = lists * BLK // HALF
    upper = span >= count
    owners = jnp.where(upper, 2 * count - 1 - span, span)
    local = jnp.where(upper, OWN_BLOCKS // 2, 0) + lists % (HALF // BLK)
    distance = ((my_index - owners) % count).reshape(-1)
    reach = BEHIND - jnp.arange(BEHIND, dtype=jnp.int32)
    block_ids = jnp.arange(OWN_BLOCKS, dtype=jnp.int32)
    wanted = jnp.any(
        (distance[:, None, None] == reach[None, :, None])
        & (local.reshape(-1)[:, None, None] == block_ids[None, None, :]),
        axis=0,
    )
    rank = jnp.cumsum(wanted.astype(jnp.int32), axis=1) - 1
    slot_ids = jnp.arange(MAX_REMOTE, dtype=jnp.int32)
    hits = wanted[:, :, None] & (rank[:, :, None] == slot_ids[None, None, :])
    chosen = jnp.sum(jnp.where(hits, block_ids[None, :, None], 0), axis=1)
    chosen_named = jnp.any(hits, axis=1)
    wraps = (reach > my_index)[:, None]
    block = jnp.where(wraps, chosen, slot_ids[None, :])
    named = jnp.where(wraps, chosen_named, wanted[:, :MAX_REMOTE])
    rows = jnp.arange(BEHIND, dtype=jnp.int32)[:, None]
    index = jnp.where(block < 2, rows * 2 + block, SLOTS + rows * 2 + block - 2)
    owner = ((my_index - reach) % count)[:, None]
    piece = jnp.where(block < 2, owner, 2 * count - 1 - owner)
    start = piece * HALF + (block % 2) * BLK
    start = jnp.where(named, start, HIDDEN)
    spread = jnp.arange(BLK, dtype=jnp.int32)
    positions = (start.reshape(-1)[:, None] + spread[None, :]).reshape(-1)
    return index.reshape(-1), positions


def attention_kernel(
    meta, key_pos, query_pos, q_raw, k_raw, v_raw, cot, weight, q_halo, far_halo, high_halo,
    two, four, six, odd, e_two, e_four, e_six, e_odd,
    dq_out, own_out, odd_out, even_out, e_odd_out, e_even_out, taps_out,
    hide, xq, xk, xv, kall, vall, kt, vt, scores, dprob, probs_half, dscore, gk, gv,
):
    my_index = meta[SLOTS]
    wrapping = my_index < BEHIND
    scale = HEAD ** -0.5
    f32 = jnp.float32
    half = jnp.bfloat16

    @pl.when(pl.program_id(0) == 0)
    def _():
        hide[...] = jnp.where(key_pos[...] <= query_pos[...], 0.0, -jnp.inf)
        gk[...] = jnp.zeros_like(gk)
        gv[...] = jnp.zeros_like(gv)

    raw = (xk, xv)
    fields = (kall, vall)
    tables = (kt, vt)
    near = {1: lambda n: odd[0, n], 3: lambda n: odd[1, n], 5: lambda n: odd[2, n],
            2: lambda n: two[n], 4: lambda n: four[n], 6: lambda n: six[n]}
    wrapped = {1: lambda n: e_odd[0, n], 3: lambda n: e_odd[1, n], 5: lambda n: e_odd[2, n],
               2: lambda n: e_two[n], 4: lambda n: e_four[n], 6: lambda n: e_six[n]}

    def convolved(x, place, which):
        base = place * RUN + PAD
        total = weight[which, 0:1, :] * x[base : base + HALF, :]
        for tap in range(1, TAPS):
            total = total + weight[which, tap : tap + 1, :] * x[base - tap : base - tap + HALF, :]
        return total.astype(half)

    def last_rows(x, place):
        return x[place * RUN + HALF : place * RUN + RUN, :]

    for side in range(2):
        xq[side * RUN : side * RUN + PAD, :] = q_halo[side]
        xq[side * RUN + PAD : (side + 1) * RUN, :] = q_raw[side * HALF : (side + 1) * HALF, :].astype(f32)
    queries = jnp.concatenate([convolved(xq, 0, 0), convolved(xq, 1, 0)], axis=0)

    own_raw = (k_raw, v_raw)
    for n in range(2):
        x = raw[n]
        for place in range(BEHIND + 1):
            base = place * RUN
            if place < BEHIND:
                rows = near[BEHIND - place](n).astype(f32)
            else:
                rows = own_raw[n][0:HALF, :].astype(f32)
            before = far_halo[n] if place == 0 else last_rows(x, place - 1)
            x[base : base + PAD, :] = jnp.where(BEHIND - place == my_index, 0.0, before)
            x[base + PAD : base + RUN, :] = rows
        base = (BEHIND + 1) * RUN
        x[base : base + PAD, :] = high_halo[n]
        x[base + PAD : base + RUN, :] = own_raw[n][HALF : 2 * HALF, :].astype(f32)
        for place in range(BEHIND):
            fields[n][place * HALF : (place + 1) * HALF, :] = convolved(x, place, n + 1)
        for side in range(2):
            first = SLOTS * BLK + side * HALF
            tables[n][first : first + HALF, :] = convolved(x, BEHIND + side, n + 1)

    @pl.when(wrapping)
    def _():
        gk[...] = jnp.zeros_like(gk)
        gv[...] = jnp.zeros_like(gv)
        for n in range(2):
            x = raw[n]
            for step in range(1, BEHIND + 1):
                place = BEHIND - step
                base = (BEHIND + 2 + place) * RUN
                before = last_rows(x, place)
                if step > 1:
                    before = jnp.where(step == my_index + 1, before, last_rows(x, BEHIND + 3 + place))
                x[base : base + PAD, :] = before
                x[base + PAD : base + RUN, :] = wrapped[step](n).astype(f32)
                first = (BEHIND + place) * HALF
                fields[n][first : first + HALF, :] = convolved(x, BEHIND + 2 + place, n + 1)

    for slot in range(SLOTS):
        source = pl.ds(pl.multiple_of(meta[slot] * BLK, BLK), BLK)
        for n in range(2):
            tables[n][slot * BLK : (slot + 1) * BLK, :] = fields[n][source, :]

    grads = cot[...]
    contract_last = (((1,), (1,)), ((), ()))
    contract_first = (((0,), (0,)), ((), ()))
    plain = (((1,), (0,)), ((), ()))
    chunk = 128
    chunks = [slice(c, c + chunk) for c in range(0, KEYS, chunk)]
    width = 2 * HALF

    def folded(x, op):
        return op(x.reshape(chunk // 8, 8, width), axis=0)

    factor = scale * math.log2(math.e)
    tops = None
    for c in chunks:
        s = lax.dot_general(kt[c, :], queries, contract_last, preferred_element_type=f32)
        s = s * factor + hide[c, :]
        scores[c, :] = s
        top = folded(s, jnp.max)
        tops = top if tops is None else jnp.maximum(tops, top)
    top = jnp.max(tops, axis=0, keepdims=True)
    totals = jnp.zeros((8, width), f32)
    for c in chunks:
        e = jnp.exp2(scores[c, :] - top)
        scores[c, :] = e
        totals = totals + folded(e, jnp.sum)
    inverse = 1.0 / jnp.sum(totals, axis=0, keepdims=True)
    deltas = jnp.zeros((8, width), f32)
    for c in chunks:
        p = scores[c, :] * inverse
        scores[c, :] = p
        pb = p.astype(half)
        probs_half[c, :] = pb
        dp = lax.dot_general(vt[c, :], grads, contract_last, preferred_element_type=f32)
        dprob[c, :] = dp
        deltas = deltas + folded(pb.astype(f32) * dp, jnp.sum)
    delta = jnp.sum(deltas, axis=0, keepdims=True)
    for number, c in enumerate(chunks):
        ds = (scores[c, :] * (dprob[c, :] - delta)).astype(half)
        dscore[c, :] = ds
        dk = lax.dot_general(ds, queries, plain, preferred_element_type=f32) * scale
        dv = lax.dot_general(probs_half[c, :], grads, plain, preferred_element_type=f32)
        for n, (out, term) in enumerate(((gk, dk), (gv, dv))):
            if c.start < SLOTS * BLK:
                for part in range(chunk // BLK):
                    slot = number * (chunk // BLK) + part
                    target = pl.ds(pl.multiple_of(meta[slot] * BLK, BLK), BLK)
                    out[target, :] = term[part * BLK : (part + 1) * BLK, :]
            else:
                first = c.start - SLOTS * BLK
                own_out[n, first : first + chunk, :] = term
    dq = lax.dot_general(dscore[...], kt[...], contract_first, preferred_element_type=f32) * scale
    dq_out[...] = dq

    def tap_sums(terms, x):
        sums = []
        for tap in range(TAPS):
            total = jnp.zeros((8, HEAD), f32)
            for rows, place in terms:
                base = place * RUN + PAD - tap
                total = total + jnp.sum((rows() * x[base : base + HALF, :]).reshape(HALF // 8, 8, HEAD), axis=0)
            sums.append(jnp.sum(total, axis=0, keepdims=True))
        return jnp.concatenate(sums, axis=0)

    taps_out[0] = tap_sums([(lambda s=s: dq_out[s * HALF : (s + 1) * HALF, :], s) for s in range(2)], xq)
    for n, g in enumerate((gk, gv)):
        terms = [(lambda p=p, g=g: g[p * HALF : (p + 1) * HALF, :], p) for p in range(BEHIND)]
        terms += [(lambda s=s, n=n: own_out[n, s * HALF : (s + 1) * HALF, :], BEHIND + s) for s in range(2)]
        taps_out[n + 1] = tap_sums(terms, raw[n])

    @pl.when(wrapping)
    def _():
        for n, g in enumerate((gk, gv)):
            terms = [
                (lambda p=p, g=g: g[(BEHIND + p) * HALF : (BEHIND + p + 1) * HALF, :], BEHIND + 2 + p)
                for p in range(BEHIND)
            ]
            taps_out[n + 1] = taps_out[n + 1] + tap_sums(terms, raw[n])

    for n, g in enumerate((gk, gv)):
        for step in range(1, BEHIND + 1):
            place = BEHIND - step
            low = g[place * HALF : (place + 1) * HALF, :]
            high = g[(BEHIND + place) * HALF : (BEHIND + place + 1) * HALF, :]
            if step % 2:
                odd_out[step // 2, n] = low.astype(half)
                e_odd_out[step // 2, n] = high.astype(half)
            else:
                even_out[step // 2 - 1, n] = low
                e_even_out[step // 2 - 1, n] = high


def attention_terms(group, heads, meta, key_pos, query_pos, tensors, weight, halos, near, wrapped):
    q_raw, k_raw, v_raw, cot = tensors
    first = group * heads
    smem = pl.BlockSpec(memory_space=pltpu.SMEM)

    def whole(shape):
        return pl.BlockSpec(shape, lambda h: (0,) * len(shape))

    def of_head(*lead):
        return pl.BlockSpec(lead + (HEAD,), lambda h: (0,) * len(lead) + (first + h,))

    def of_group(*lead):
        return pl.BlockSpec(lead + (HEAD,), lambda h: (0,) * len(lead) + (h,))

    rows = 2 * HALF
    channels = heads * HEAD
    f32 = jnp.float32
    half = jnp.bfloat16
    piece = of_group(2, HALF)
    pieces = of_group(3, 2, HALF)
    run = functools.partial(pltpu.VMEM)
    return pl.pallas_call(
        attention_kernel,
        grid=(heads,),
        in_specs=[
            smem, whole((KEYS, 1)), whole((1, rows)),
            of_head(rows), of_head(rows), of_head(rows), of_head(rows),
            of_head(3, TAPS), of_head(2, PAD), of_head(2, PAD), of_head(2, PAD),
            piece, piece, piece, pieces, piece, piece, piece, pieces,
        ],
        out_specs=[of_group(rows), of_group(2, rows), pieces, pieces, pieces, pieces, of_group(3, TAPS)],
        out_shape=[
            jax.ShapeDtypeStruct((rows, channels), f32),
            jax.ShapeDtypeStruct((2, rows, channels), f32),
            jax.ShapeDtypeStruct((3, 2, HALF, channels), half),
            jax.ShapeDtypeStruct((3, 2, HALF, channels), f32),
            jax.ShapeDtypeStruct((3, 2, HALF, channels), half),
            jax.ShapeDtypeStruct((3, 2, HALF, channels), f32),
            jax.ShapeDtypeStruct((3, TAPS, channels), f32),
        ],
        scratch_shapes=[
            run((KEYS, rows), f32),
            run((2 * RUN, HEAD), f32),
            run((14 * RUN, HEAD), f32), run((14 * RUN, HEAD), f32),
            run((2 * BEHIND * HALF, HEAD), half), run((2 * BEHIND * HALF, HEAD), half),
            run((KEYS, HEAD), half), run((KEYS, HEAD), half),
            run((KEYS, rows), f32), run((KEYS, rows), f32),
            run((KEYS, rows), half), run((KEYS, rows), half),
            run((2 * BEHIND * HALF, HEAD), f32), run((2 * BEHIND * HALF, HEAD), f32),
        ],
        compiler_params=pltpu.CompilerParams(vmem_limit_bytes=VMEM),
        cost_estimate=pl.CostEstimate(
            flops=heads * 100 * rows * KEYS * HEAD, bytes_accessed=heads * 3 * 1024 * 1024, transcendentals=heads * rows * KEYS
        ),
        name="attention",
    )(meta, key_pos, query_pos, q_raw, k_raw, v_raw, cot, weight, *halos, *near, *wrapped)


def unconvolved(rows, after, taps):
    extended = jnp.concatenate([rows, after], axis=0)
    total = taps[0:1, :] * extended[:HALF, :]
    for tap in range(1, TAPS):
        total = total + taps[tap : tap + 1, :] * extended[tap : tap + HALF, :]
    return total.astype(jnp.bfloat16)


def query_kernel(grad, after, weight, out):
    for side in range(2):
        rows = slice(side * HALF, (side + 1) * HALF)
        out[rows, :] = unconvolved(grad[rows, :], after[side], weight[0])


def final_kernel(terms, meta, own, beside, after, weight, *rest):
    outs = rest[-2:]
    sent = rest[:terms]
    e_sent = rest[terms : terms + 2]
    f32 = jnp.float32
    first_core = meta[0] % 2 == 0
    for n in range(2):
        low = own[n, 0:HALF, :] + jnp.where(first_core, beside[0, n].astype(f32), 0.0)
        for x in sent:
            low = low + x[n].astype(f32)
        high = own[n, HALF : 2 * HALF, :]
        for x in e_sent:
            high = high + x[n].astype(f32)
        outs[n][0:HALF, :] = unconvolved(low, after[n, 0], weight[n + 1])
        outs[n][HALF : 2 * HALF, :] = unconvolved(high, after[n, 1], weight[n + 1])


def combine_kernel(meta, even, odd, e_even, e_odd, two, four, six, e_two, e_four, e_six):
    f32 = jnp.float32
    first_core = meta[0] % 2 == 0
    for evens, odds, outs in ((even, odd, (two, four, six)), (e_even, e_odd, (e_two, e_four, e_six))):
        for n in range(2):
            wide = [odds[m, n].astype(f32) for m in range(3)]
            beside = [
                jnp.where(first_core, wide[1], wide[0]),
                jnp.where(first_core, wide[2], wide[1]),
                jnp.where(first_core, 0.0, wide[2]),
            ]
            for m, out in enumerate(outs):
                out[n] = (evens[m, n] + beside[m]).astype(out.dtype)


def combined(meta, even, odd, e_even, e_odd):
    channels = even.shape[-1]
    wide = min(WIDE, channels)
    half = jnp.bfloat16
    f32 = jnp.float32
    pieces = pl.BlockSpec((3, 2, HALF, wide), lambda h: (0, 0, 0, h))
    piece = pl.BlockSpec((2, HALF, wide), lambda h: (0, 0, h))
    types = [half] * 5 + [f32]
    return pl.pallas_call(
        combine_kernel,
        grid=(channels // wide,),
        in_specs=[pl.BlockSpec(memory_space=pltpu.SMEM)] + [pieces] * 4,
        out_specs=[piece] * 6,
        out_shape=[jax.ShapeDtypeStruct((2, HALF, channels), t) for t in types],
        compiler_params=pltpu.CompilerParams(vmem_limit_bytes=VMEM),
        name="combine",
    )(meta, even, odd, e_even, e_odd)


def finished(group, heads, meta, own, near, beside, wrapped, after, weight, earlier):
    rows = 2 * HALF
    channels = heads * HEAD
    wide = min(WIDE, channels)
    first = group * (channels // wide)

    def of_group(*lead):
        return pl.BlockSpec(lead + (wide,), lambda h: (0,) * len(lead) + (h,))

    def of_head(*lead):
        return pl.BlockSpec(lead + (wide,), lambda h: (0,) * len(lead) + (first + h,))

    piece = of_group(2, HALF)
    anywhere = pl.BlockSpec(memory_space=pl.ANY)
    shape = jax.ShapeDtypeStruct((rows, GROUPS * channels), jnp.bfloat16)
    extra = [] if earlier is None else list(earlier)
    terms = len(near) + len(wrapped)
    return pl.pallas_call(
        functools.partial(final_kernel, len(near)),
        grid=(channels // wide,),
        in_specs=[
            pl.BlockSpec(memory_space=pltpu.SMEM), of_group(2, rows), of_group(1, 2, HALF),
            of_head(2, 2, PAD), of_head(3, TAPS),
        ]
        + [piece] * terms
        + [anywhere] * len(extra),
        out_specs=[of_head(rows), of_head(rows)],
        out_shape=[shape, shape],
        input_output_aliases={5 + terms + n: n for n in range(len(extra))},
        compiler_params=pltpu.CompilerParams(vmem_limit_bytes=VMEM),
        name="finish",
    )(meta, own, beside, after, weight, *near, *wrapped, *extra)


def body(query_in, key_in, value_in, conv_weight, out_grad, block_lists):
    q_raw, k_raw, v_raw, cot = (x[0] for x in (query_in, key_in, value_in, out_grad))
    f32 = jnp.float32
    half = jnp.bfloat16
    channels = q_raw.shape[1]
    rows = 2 * HALF
    heads = channels // HEAD // GROUPS
    width = heads * HEAD
    count = lax.axis_size("ctx")
    my_index = lax.axis_index("ctx")
    first_core = my_index % 2 == 0
    is_last = my_index == count - 1
    up = [(i, i + 1) for i in range(count - 1)]
    down = [(i + 1, i) for i in range(count - 1)]
    every = sibling_pairs(count)
    few = sibling_pairs(BEHIND)

    tail = slice(HALF - PAD, HALF)
    high_tail = slice(rows - PAD, rows)
    q_before = along(q_raw[tail], up)
    far = along(jnp.stack([k_raw[tail], v_raw[tail]]), ring_pairs(count, BEHIND + 1))
    above = along(jnp.stack([x[high_tail] for x in (q_raw, k_raw, v_raw)]), down)

    near = []
    wrapped = []
    for group in range(GROUPS):
        part = slice(group * width, (group + 1) * width)
        low = jnp.stack([k_raw[:HALF, part], v_raw[:HALF, part]])
        high = jnp.stack([k_raw[HALF:, part], v_raw[HALF:, part]])
        if group:
            low, high = once((low, high), ready)
        two = along(low, ring_pairs(count, 2))
        six = along(low, ring_pairs(count, 6))
        if group == 0:
            ready = once(six, q_before, far, above)
            four = along(ready, ring_pairs(count, -2))
        else:
            four = along(low, ring_pairs(count, 4))
        e_two = along(high, wrapped_out(count, 2))
        e_six = along(high, wrapped_out(count, 6))
        near.append((two, four, six, low))
        wrapped.append((e_two, e_six, high))

    below = jnp.stack([x[tail] for x in (q_raw, k_raw, v_raw)])
    above = jnp.where(is_last, below, above).astype(f32)
    q_halo = jnp.stack([q_before.astype(f32), above[0]])
    halos = (q_halo, far.astype(f32), above[1:])

    index, remote_pos = table_of_slots(block_lists[0], my_index, count)
    spread = jnp.arange(HALF, dtype=jnp.int32)
    positions = jnp.concatenate([my_index * HALF + spread, (2 * count - 1 - my_index) * HALF + spread])
    key_pos = jnp.concatenate([remote_pos, positions])[:, None]
    place = my_index[None].astype(jnp.int32)
    meta = jnp.concatenate([index, place]).astype(jnp.int32)

    steps = exchange_steps(("ctx", "dp"))
    results = []
    returned = []
    for group in range(GROUPS):
        two, four, six, low = near[group]
        e_two, e_six, high = wrapped[group]
        if group:
            low, high, e_six = once((low, high, e_six), results[-1][6])
        else:
            low, high = once((low, high), near[1][0])
        e_four = along(e_six, [(i + 2, i) for i in range(4)])
        beside = shared(low, two, four, six, first_core, every)
        e_beside = shared(high, e_two, e_four, e_six, first_core, few)
        result = attention_terms(
            group, heads, meta, key_pos, positions[None, :], (q_raw, k_raw, v_raw, cot), conv_weight, halos,
            (two, four, six, beside), (e_two, e_four, e_six, e_beside),
        )
        _, _, odd, even, e_odd, e_even, _ = result
        if group:
            odd, e_odd = once((odd, e_odd), *returned[-1][0], returned[-1][2][0], e_merged)
        got = along(odd, every)
        e_got = along(e_odd, few)
        if group:
            kernel_terms = exchanged(jnp.concatenate([r[6] for r in (*results, result)], axis=2), steps[:2])
            got, e_got = once((got, e_got), kernel_terms)
        two, four, six, e_two, e_four, e_six = combined(place, even, got, e_even, e_got)
        meta = once(meta, two)
        sent_two = along(two, ring_pairs(count, -2))
        sent_four = along(four, ring_pairs(count, -4))
        sent_six = along(six, ring_pairs(count, -6))
        e_sent_two = along(e_two, wrapped_back(count, 2))
        e_six = (e_six + along(e_four, [(i, i + 2) for i in range(4)]).astype(f32)).astype(half)
        e_merged = e_six
        e_sent_six = along(e_six, wrapped_back(count, 6))
        results.append(result)
        returned.append(((sent_two, sent_four, sent_six), got, (e_sent_two, e_sent_six)))

    kernel_grad = exchanged(once(kernel_terms, sent_two, sent_four, sent_six, e_sent_two, e_merged), steps[2:])

    def after_rows(heads_of):
        low, high = heads_of
        next_low = along(low, down)
        next_high = along(high, up)
        return jnp.stack([jnp.where(is_last, high, next_low), next_high], axis=-3)

    dq = once(jnp.concatenate([r[0] for r in results], axis=1), sent_two, sent_six)
    q_after = after_rows((dq[:PAD], dq[HALF : HALF + PAD]))
    wide = min(WIDE, width)
    spec = pl.BlockSpec((rows, wide), lambda h: (0, h))
    query_grad = pl.pallas_call(
        query_kernel,
        grid=(channels // wide,),
        in_specs=[
            spec,
            pl.BlockSpec((2, PAD, wide), lambda h: (0, 0, h)),
            pl.BlockSpec((3, TAPS, wide), lambda h: (0, 0, h)),
        ],
        out_specs=spec,
        out_shape=jax.ShapeDtypeStruct((rows, channels), half),
        compiler_params=pltpu.CompilerParams(vmem_limit_bytes=VMEM),
        name="query_finish",
    )(dq, q_after, conv_weight)

    lows = []
    highs = []
    for group in range(GROUPS):
        own = results[group][1]
        sent, got, e_sent = returned[group]
        low = own[:, :PAD] + jnp.where(first_core, got[0, :, :PAD].astype(f32), 0.0)
        high = own[:, HALF : HALF + PAD]
        for x in sent:
            low = low + x[:, :PAD].astype(f32)
        for x in e_sent:
            high = high + x[:, :PAD].astype(f32)
        lows.append(low)
        highs.append(high)
    after = after_rows((jnp.concatenate(lows, axis=2), jnp.concatenate(highs, axis=2)))
    outs = None
    for group in range(GROUPS):
        sent, got, e_sent = returned[group]
        outs = finished(group, heads, place, results[group][1], sent, got, e_sent, after, conv_weight, outs)
    return (query_grad[None], outs[0][None], outs[1][None], kernel_grad)


def solution(mesh):
    placed = (
        P("dp", "ctx", None),
        P("dp", "ctx", None),
        P("dp", "ctx", None),
        P(),
        P("dp", "ctx", None),
        P("dp", "ctx", None),
    )
    return jax.shard_map(
        body,
        mesh=mesh,
        in_specs=placed,
        out_specs=(P("dp", "ctx", None), P("dp", "ctx", None), P("dp", "ctx", None), P()),
        check_vma=False,
    )
```

```python
import functools
import math

import jax
import jax.numpy as jnp
from jax import lax
from jax.experimental import pallas as pl
from jax.experimental.pallas import tpu as pltpu
from jax.sharding import PartitionSpec as P

HEAD = 128
TAPS = 4
BLK = 64
BEHIND = 6
MAX_REMOTE = 2
HALF = 128
OWN_BLOCKS = 4
PAD = 8
RUN = HALF + PAD
SLOTS = BEHIND * MAX_REMOTE
KEYS = SLOTS * BLK + 2 * HALF
GROUPS = 2
HIDDEN = 1 << 30
WIDE = 512
VMEM = 48 * 1024 * 1024


def along(x, pairs):
    return lax.ppermute(x, "ctx", pairs)


def ring_pairs(count, by):
    return [(i, (i + by) % count) for i in range(count)]


def sibling_pairs(count):
    return [(i, i ^ 1) for i in range(count)]


def wrapped_out(count, by):
    return [(i, i + by - count) for i in range(count - by, count)]


def wrapped_back(count, by):
    return [(j, i) for i, j in wrapped_out(count, by)]


def once(x, *others):
    return lax.optimization_barrier((x, others))[0]


def exchange_steps(axes):
    steps = []
    for axis in axes:
        step = 1
        while step < lax.axis_size(axis):
            steps.append((axis, step))
            step *= 4
    return steps


def exchanged(x, axis, step):
    count = lax.axis_size(axis)
    others = [lax.ppermute(x, axis, [(i, i ^ (step * k)) for i in range(count)]) for k in range(1, 4)]
    return (x + others[0]) + (others[1] + others[2])


def shared(own, from_two, from_four, from_six, first_core, pairs):
    mine = jnp.stack(
        [
            jnp.where(first_core, own, from_two),
            jnp.where(first_core, from_two, from_four),
            jnp.where(first_core, from_four, from_six),
        ]
    )
    return along(mine, pairs)


def table_of_slots(lists, my_index, count):
    span = lists * BLK // HALF
    upper = span >= count
    owners = jnp.where(upper, 2 * count - 1 - span, span)
    local = jnp.where(upper, OWN_BLOCKS // 2, 0) + lists % (HALF // BLK)
    distance = ((my_index - owners) % count).reshape(-1)
    reach = BEHIND - jnp.arange(BEHIND, dtype=jnp.int32)
    block_ids = jnp.arange(OWN_BLOCKS, dtype=jnp.int32)
    wanted = jnp.any(
        (distance[:, None, None] == reach[None, :, None])
        & (local.reshape(-1)[:, None, None] == block_ids[None, None, :]),
        axis=0,
    )
    rank = jnp.cumsum(wanted.astype(jnp.int32), axis=1) - 1
    slot_ids = jnp.arange(MAX_REMOTE, dtype=jnp.int32)
    hits = wanted[:, :, None] & (rank[:, :, None] == slot_ids[None, None, :])
    chosen = jnp.sum(jnp.where(hits, block_ids[None, :, None], 0), axis=1)
    chosen_named = jnp.any(hits, axis=1)
    wraps = (reach > my_index)[:, None]
    block = jnp.where(wraps, chosen, slot_ids[None, :])
    named = jnp.where(wraps, chosen_named, wanted[:, :MAX_REMOTE])
    rows = jnp.arange(BEHIND, dtype=jnp.int32)[:, None]
    index = jnp.where(block < 2, rows * 2 + block, SLOTS + rows * 2 + block - 2)
    owner = ((my_index - reach) % count)[:, None]
    piece = jnp.where(block < 2, owner, 2 * count - 1 - owner)
    start = piece * HALF + (block % 2) * BLK
    start = jnp.where(named, start, HIDDEN)
    spread = jnp.arange(BLK, dtype=jnp.int32)
    positions = (start.reshape(-1)[:, None] + spread[None, :]).reshape(-1)
    return index.reshape(-1), positions


def attention_kernel(
    meta, key_pos, query_pos, q_raw, k_raw, v_raw, cot, weight, q_halo, far_halo, high_halo,
    two, four, six, odd, e_two, e_four, e_six, e_odd,
    dq_out, own_out, odd_out, even_out, e_odd_out, e_even_out, taps_out,
    hide, xq, xk, xv, kall, vall, kt, vt, scores, dprob, probs_half, dscore, gk, gv,
):
    my_index = meta[SLOTS]
    wrapping = my_index < BEHIND
    scale = HEAD ** -0.5
    f32 = jnp.float32
    half = jnp.bfloat16

    @pl.when(pl.program_id(0) == 0)
    def _():
        hide[...] = jnp.where(key_pos[...] <= query_pos[...], 0.0, -jnp.inf)
        gk[...] = jnp.zeros_like(gk)
        gv[...] = jnp.zeros_like(gv)

    raw = (xk, xv)
    fields = (kall, vall)
    tables = (kt, vt)
    near = {1: lambda n: odd[0, n], 3: lambda n: odd[1, n], 5: lambda n: odd[2, n],
            2: lambda n: two[n], 4: lambda n: four[n], 6: lambda n: six[n]}
    wrapped = {1: lambda n: e_odd[0, n], 3: lambda n: e_odd[1, n], 5: lambda n: e_odd[2, n],
               2: lambda n: e_two[n], 4: lambda n: e_four[n], 6: lambda n: e_six[n]}

    def convolved(x, place, which):
        base = place * RUN + PAD
        total = weight[which, 0:1, :] * x[base : base + HALF, :]
        for tap in range(1, TAPS):
            total = total + weight[which, tap : tap + 1, :] * x[base - tap : base - tap + HALF, :]
        return total.astype(half)

    def last_rows(x, place):
        return x[place * RUN + HALF : place * RUN + RUN, :]

    for side in range(2):
        xq[side * RUN : side * RUN + PAD, :] = q_halo[side]
        xq[side * RUN + PAD : (side + 1) * RUN, :] = q_raw[side * HALF : (side + 1) * HALF, :].astype(f32)
    queries = jnp.concatenate([convolved(xq, 0, 0), convolved(xq, 1, 0)], axis=0)

    own_raw = (k_raw, v_raw)
    for n in range(2):
        x = raw[n]
        for place in range(BEHIND + 1):
            base = place * RUN
            if place < BEHIND:
                rows = near[BEHIND - place](n).astype(f32)
            else:
                rows = own_raw[n][0:HALF, :].astype(f32)
            before = far_halo[n] if place == 0 else last_rows(x, place - 1)
            x[base : base + PAD, :] = jnp.where(BEHIND - place == my_index, 0.0, before)
            x[base + PAD : base + RUN, :] = rows
        base = (BEHIND + 1) * RUN
        x[base : base + PAD, :] = high_halo[n]
        x[base + PAD : base + RUN, :] = own_raw[n][HALF : 2 * HALF, :].astype(f32)
        for place in range(BEHIND):
            fields[n][place * HALF : (place + 1) * HALF, :] = convolved(x, place, n + 1)
        for side in range(2):
            first = SLOTS * BLK + side * HALF
            tables[n][first : first + HALF, :] = convolved(x, BEHIND + side, n + 1)

    @pl.when(wrapping)
    def _():
        gk[...] = jnp.zeros_like(gk)
        gv[...] = jnp.zeros_like(gv)
        for n in range(2):
            x = raw[n]
            for step in range(1, BEHIND + 1):
                place = BEHIND - step
                base = (BEHIND + 2 + place) * RUN
                before = last_rows(x, place)
                if step > 1:
                    before = jnp.where(step == my_index + 1, before, last_rows(x, BEHIND + 3 + place))
                x[base : base + PAD, :] = before
                x[base + PAD : base + RUN, :] = wrapped[step](n).astype(f32)
                first = (BEHIND + place) * HALF
                fields[n][first : first + HALF, :] = convolved(x, BEHIND + 2 + place, n + 1)

    for slot in range(SLOTS):
        source = pl.ds(pl.multiple_of(meta[slot] * BLK, BLK), BLK)
        for n in range(2):
            tables[n][slot * BLK : (slot + 1) * BLK, :] = fields[n][source, :]

    grads = cot[...]
    contract_last = (((1,), (1,)), ((), ()))
    contract_first = (((0,), (0,)), ((), ()))
    plain = (((1,), (0,)), ((), ()))
    chunk = 128
    chunks = [slice(c, c + chunk) for c in range(0, KEYS, chunk)]
    width = 2 * HALF

    def folded(x, op):
        return op(x.reshape(chunk // 8, 8, width), axis=0)

    factor = scale * math.log2(math.e)
    tops = None
    for c in chunks:
        s = lax.dot_general(kt[c, :], queries, contract_last, preferred_element_type=f32)
        s = s * factor + hide[c, :]
        scores[c, :] = s
        top = folded(s, jnp.max)
        tops = top if tops is None else jnp.maximum(tops, top)
    top = jnp.max(tops, axis=0, keepdims=True)
    totals = jnp.zeros((8, width), f32)
    for c in chunks:
        e = jnp.exp2(scores[c, :] - top)
        scores[c, :] = e
        totals = totals + folded(e, jnp.sum)
    inverse = 1.0 / jnp.sum(totals, axis=0, keepdims=True)
    deltas = jnp.zeros((8, width), f32)
    for c in chunks:
        p = scores[c, :] * inverse
        scores[c, :] = p
        pb = p.astype(half)
        probs_half[c, :] = pb
        dp = lax.dot_general(vt[c, :], grads, contract_last, preferred_element_type=f32)
        dprob[c, :] = dp
        deltas = deltas + folded(pb.astype(f32) * dp, jnp.sum)
    delta = jnp.sum(deltas, axis=0, keepdims=True)
    for number, c in enumerate(chunks):
        ds = (scores[c, :] * (dprob[c, :] - delta)).astype(half)
        dscore[c, :] = ds
        dk = lax.dot_general(ds, queries, plain, preferred_element_type=f32) * scale
        dv = lax.dot_general(probs_half[c, :], grads, plain, preferred_element_type=f32)
        for n, (out, term) in enumerate(((gk, dk), (gv, dv))):
            if c.start < SLOTS * BLK:
                for part in range(chunk // BLK):
                    slot = number * (chunk // BLK) + part
                    target = pl.ds(pl.multiple_of(meta[slot] * BLK, BLK), BLK)
                    out[target, :] = term[part * BLK : (part + 1) * BLK, :]
            else:
                first = c.start - SLOTS * BLK
                own_out[n, first : first + chunk, :] = term
    dq = lax.dot_general(dscore[...], kt[...], contract_first, preferred_element_type=f32) * scale
    dq_out[...] = dq

    def tap_sums(terms, x):
        sums = []
        for tap in range(TAPS):
            total = jnp.zeros((8, HEAD), f32)
            for rows, place in terms:
                base = place * RUN + PAD - tap
                total = total + jnp.sum((rows() * x[base : base + HALF, :]).reshape(HALF // 8, 8, HEAD), axis=0)
            sums.append(jnp.sum(total, axis=0, keepdims=True))
        return jnp.concatenate(sums, axis=0)

    taps_out[0] = tap_sums([(lambda s=s: dq_out[s * HALF : (s + 1) * HALF, :], s) for s in range(2)], xq)
    for n, g in enumerate((gk, gv)):
        terms = [(lambda p=p, g=g: g[p * HALF : (p + 1) * HALF, :], p) for p in range(BEHIND)]
        terms += [(lambda s=s, n=n: own_out[n, s * HALF : (s + 1) * HALF, :], BEHIND + s) for s in range(2)]
        taps_out[n + 1] = tap_sums(terms, raw[n])

    @pl.when(wrapping)
    def _():
        for n, g in enumerate((gk, gv)):
            terms = [
                (lambda p=p, g=g: g[(BEHIND + p) * HALF : (BEHIND + p + 1) * HALF, :], BEHIND + 2 + p)
                for p in range(BEHIND)
            ]
            taps_out[n + 1] = taps_out[n + 1] + tap_sums(terms, raw[n])

    for n, g in enumerate((gk, gv)):
        for step in range(1, BEHIND + 1):
            place = BEHIND - step
            low = g[place * HALF : (place + 1) * HALF, :]
            high = g[(BEHIND + place) * HALF : (BEHIND + place + 1) * HALF, :]
            if step % 2:
                odd_out[step // 2, n] = low.astype(half)
                e_odd_out[step // 2, n] = high.astype(half)
            else:
                even_out[step // 2 - 1, n] = low
                e_even_out[step // 2 - 1, n] = high


def attention_terms(group, heads, meta, key_pos, query_pos, tensors, weight, halos, near, wrapped):
    q_raw, k_raw, v_raw, cot = tensors
    first = group * heads
    smem = pl.BlockSpec(memory_space=pltpu.SMEM)

    def whole(shape):
        return pl.BlockSpec(shape, lambda h: (0,) * len(shape))

    def of_head(*lead):
        return pl.BlockSpec(lead + (HEAD,), lambda h: (0,) * len(lead) + (first + h,))

    def of_group(*lead):
        return pl.BlockSpec(lead + (HEAD,), lambda h: (0,) * len(lead) + (h,))

    rows = 2 * HALF
    channels = heads * HEAD
    f32 = jnp.float32
    half = jnp.bfloat16
    piece = of_group(2, HALF)
    pieces = of_group(3, 2, HALF)
    run = functools.partial(pltpu.VMEM)
    return pl.pallas_call(
        attention_kernel,
        grid=(heads,),
        in_specs=[
            smem, whole((KEYS, 1)), whole((1, rows)),
            of_head(rows), of_head(rows), of_head(rows), of_head(rows),
            of_head(3, TAPS), of_head(2, PAD), of_head(2, PAD), of_head(2, PAD),
            piece, piece, piece, pieces, piece, piece, piece, pieces,
        ],
        out_specs=[of_group(rows), of_group(2, rows), pieces, pieces, pieces, pieces, of_group(3, TAPS)],
        out_shape=[
            jax.ShapeDtypeStruct((rows, channels), f32),
            jax.ShapeDtypeStruct((2, rows, channels), f32),
            jax.ShapeDtypeStruct((3, 2, HALF, channels), half),
            jax.ShapeDtypeStruct((3, 2, HALF, channels), f32),
            jax.ShapeDtypeStruct((3, 2, HALF, channels), half),
            jax.ShapeDtypeStruct((3, 2, HALF, channels), f32),
            jax.ShapeDtypeStruct((3, TAPS, channels), f32),
        ],
        scratch_shapes=[
            run((KEYS, rows), f32),
            run((2 * RUN, HEAD), f32),
            run((14 * RUN, HEAD), f32), run((14 * RUN, HEAD), f32),
            run((2 * BEHIND * HALF, HEAD), half), run((2 * BEHIND * HALF, HEAD), half),
            run((KEYS, HEAD), half), run((KEYS, HEAD), half),
            run((KEYS, rows), f32), run((KEYS, rows), f32),
            run((KEYS, rows), half), run((KEYS, rows), half),
            run((2 * BEHIND * HALF, HEAD), f32), run((2 * BEHIND * HALF, HEAD), f32),
        ],
        compiler_params=pltpu.CompilerParams(vmem_limit_bytes=VMEM),
        cost_estimate=pl.CostEstimate(
            flops=heads * 100 * rows * KEYS * HEAD, bytes_accessed=heads * 3 * 1024 * 1024, transcendentals=heads * rows * KEYS
        ),
        name="attention",
    )(meta, key_pos, query_pos, q_raw, k_raw, v_raw, cot, weight, *halos, *near, *wrapped)


def unconvolved(rows, after, taps):
    extended = jnp.concatenate([rows, after], axis=0)
    total = taps[0:1, :] * extended[:HALF, :]
    for tap in range(1, TAPS):
        total = total + taps[tap : tap + 1, :] * extended[tap : tap + HALF, :]
    return total.astype(jnp.bfloat16)


def query_kernel(grad, after, weight, out):
    for side in range(2):
        rows = slice(side * HALF, (side + 1) * HALF)
        out[rows, :] = unconvolved(grad[rows, :], after[side], weight[0])


def final_kernel(terms, meta, own, beside, after, weight, *rest):
    outs = rest[-2:]
    sent = rest[:terms]
    e_sent = rest[terms : terms + 2]
    f32 = jnp.float32
    first_core = meta[0] % 2 == 0
    for n in range(2):
        low = own[n, 0:HALF, :] + jnp.where(first_core, beside[0, n].astype(f32), 0.0)
        for x in sent:
            low = low + x[n].astype(f32)
        high = own[n, HALF : 2 * HALF, :]
        for x in e_sent:
            high = high + x[n].astype(f32)
        outs[n][0:HALF, :] = unconvolved(low, after[n, 0], weight[n + 1])
        outs[n][HALF : 2 * HALF, :] = unconvolved(high, after[n, 1], weight[n + 1])


def combine_kernel(meta, even, odd, e_even, e_odd, two, four, six, e_two, e_four, e_six):
    f32 = jnp.float32
    first_core = meta[0] % 2 == 0
    for evens, odds, outs in ((even, odd, (two, four, six)), (e_even, e_odd, (e_two, e_four, e_six))):
        for n in range(2):
            wide = [odds[m, n].astype(f32) for m in range(3)]
            beside = [
                jnp.where(first_core, wide[1], wide[0]),
                jnp.where(first_core, wide[2], wide[1]),
                jnp.where(first_core, 0.0, wide[2]),
            ]
            for m, out in enumerate(outs):
                out[n] = (evens[m, n] + beside[m]).astype(out.dtype)


def combined(meta, even, odd, e_even, e_odd):
    channels = even.shape[-1]
    wide = min(WIDE, channels)
    half = jnp.bfloat16
    f32 = jnp.float32
    pieces = pl.BlockSpec((3, 2, HALF, wide), lambda h: (0, 0, 0, h))
    piece = pl.BlockSpec((2, HALF, wide), lambda h: (0, 0, h))
    types = [half] * 5 + [f32]
    return pl.pallas_call(
        combine_kernel,
        grid=(channels // wide,),
        in_specs=[pl.BlockSpec(memory_space=pltpu.SMEM)] + [pieces] * 4,
        out_specs=[piece] * 6,
        out_shape=[jax.ShapeDtypeStruct((2, HALF, channels), t) for t in types],
        compiler_params=pltpu.CompilerParams(vmem_limit_bytes=VMEM),
        name="combine",
    )(meta, even, odd, e_even, e_odd)


def finished(group, heads, meta, own, near, beside, wrapped, after, weight, earlier):
    rows = 2 * HALF
    channels = heads * HEAD
    wide = min(WIDE, channels)
    first = group * (channels // wide)

    def of_group(*lead):
        return pl.BlockSpec(lead + (wide,), lambda h: (0,) * len(lead) + (h,))

    def of_head(*lead):
        return pl.BlockSpec(lead + (wide,), lambda h: (0,) * len(lead) + (first + h,))

    piece = of_group(2, HALF)
    anywhere = pl.BlockSpec(memory_space=pl.ANY)
    shape = jax.ShapeDtypeStruct((rows, GROUPS * channels), jnp.bfloat16)
    extra = [] if earlier is None else list(earlier)
    terms = len(near) + len(wrapped)
    return pl.pallas_call(
        functools.partial(final_kernel, len(near)),
        grid=(channels // wide,),
        in_specs=[
            pl.BlockSpec(memory_space=pltpu.SMEM), of_group(2, rows), of_group(1, 2, HALF),
            of_head(2, 2, PAD), of_head(3, TAPS),
        ]
        + [piece] * terms
        + [anywhere] * len(extra),
        out_specs=[of_head(rows), of_head(rows)],
        out_shape=[shape, shape],
        input_output_aliases={5 + terms + n: n for n in range(len(extra))},
        compiler_params=pltpu.CompilerParams(vmem_limit_bytes=VMEM),
        name="finish",
    )(meta, own, beside, after, weight, *near, *wrapped, *extra)


def body(query_in, key_in, value_in, conv_weight, out_grad, block_lists):
    q_raw, k_raw, v_raw, cot = (x[0] for x in (query_in, key_in, value_in, out_grad))
    f32 = jnp.float32
    half = jnp.bfloat16
    channels = q_raw.shape[1]
    rows = 2 * HALF
    heads = channels // HEAD // GROUPS
    width = heads * HEAD
    count = lax.axis_size("ctx")
    my_index = lax.axis_index("ctx")
    first_core = my_index % 2 == 0
    is_last = my_index == count - 1
    up = [(i, i + 1) for i in range(count - 1)]
    down = [(i + 1, i) for i in range(count - 1)]
    every = sibling_pairs(count)
    few = sibling_pairs(BEHIND)

    tail = slice(HALF - PAD, HALF)
    high_tail = slice(rows - PAD, rows)
    q_before = along(q_raw[tail], up)
    far = along(jnp.stack([k_raw[tail], v_raw[tail]]), ring_pairs(count, BEHIND + 1))
    above = along(jnp.stack([x[high_tail] for x in (q_raw, k_raw, v_raw)]), down)

    near = []
    wrapped = []
    for group in range(GROUPS):
        part = slice(group * width, (group + 1) * width)
        low = jnp.stack([k_raw[:HALF, part], v_raw[:HALF, part]])
        high = jnp.stack([k_raw[HALF:, part], v_raw[HALF:, part]])
        if group:
            low, high = once((low, high), ready)
        two = along(low, ring_pairs(count, 2))
        six = along(low, ring_pairs(count, 6))
        if group == 0:
            ready = once(six, q_before, far, above)
            four = along(ready, ring_pairs(count, -2))
        else:
            four = along(low, ring_pairs(count, 4))
        e_two = along(high, wrapped_out(count, 2))
        e_six = along(high, wrapped_out(count, 6))
        near.append((two, four, six, low))
        wrapped.append((e_two, e_six, high))

    below = jnp.stack([x[tail] for x in (q_raw, k_raw, v_raw)])
    above = jnp.where(is_last, below, above).astype(f32)
    q_halo = jnp.stack([q_before.astype(f32), above[0]])
    halos = (q_halo, far.astype(f32), above[1:])

    index, remote_pos = table_of_slots(block_lists[0], my_index, count)
    spread = jnp.arange(HALF, dtype=jnp.int32)
    positions = jnp.concatenate([my_index * HALF + spread, (2 * count - 1 - my_index) * HALF + spread])
    key_pos = jnp.concatenate([remote_pos, positions])[:, None]
    place = my_index[None].astype(jnp.int32)
    meta = jnp.concatenate([index, place]).astype(jnp.int32)

    def after_rows(heads_of):
        low, high = heads_of
        next_low = along(low, down)
        next_high = along(high, up)
        return jnp.stack([jnp.where(is_last, high, next_low), next_high], axis=-3)

    steps = exchange_steps(("ctx", "dp"))
    results = []
    returned = []
    joining = []

    def joined(e_six, e_four, after):
        e_four = once(e_four, after)
        return along((e_six + e_four.astype(f32)).astype(half), wrapped_back(count, 6))

    for group in range(GROUPS):
        two, four, six, low = near[group]
        e_two, e_six, high = wrapped[group]
        if group:
            low, high, e_six = once((low, high, e_six), results[-1][6])
        else:
            low, high = once((low, high), near[1][0])
        e_four = along(e_six, [(i + 2, i) for i in range(4)])
        beside = shared(low, two, four, six, first_core, every)
        e_beside = shared(high, e_two, e_four, e_six, first_core, few)
        result = attention_terms(
            group, heads, meta, key_pos, positions[None, :], (q_raw, k_raw, v_raw, cot), conv_weight, halos,
            (two, four, six, beside), (e_two, e_four, e_six, e_beside),
        )
        _, _, odd, even, e_odd, e_even, _ = result
        if group:
            e_sent_six = [joined(*joining[0], result[6])]
            odd, e_odd = once((odd, e_odd), *returned[-1][0], returned[-1][2], joining[0][1])
        got = along(odd, every)
        e_got = along(e_odd, few)
        if group:
            kernel_terms = exchanged(jnp.concatenate([r[6] for r in (*results, result)], axis=2), *steps[0])
            dq = jnp.concatenate([r[0] for r in (*results, result)], axis=1)
            q_after = after_rows((dq[:PAD], dq[HALF : HALF + PAD]))
            got, e_got = once((got, e_got), kernel_terms, q_after)
        two, four, six, e_two, e_four, e_six = combined(place, even, got, e_even, e_got)
        meta = once(meta, two)
        sent_two = along(two, ring_pairs(count, -2))
        sent_four = along(four, ring_pairs(count, -4))
        sent_six = along(six, ring_pairs(count, -6))
        e_sent_two = along(e_two, wrapped_back(count, 2))
        joining.append((e_six, along(e_four, [(i, i + 2) for i in range(4)])))
        results.append(result)
        returned.append(((sent_two, sent_four, sent_six), got, e_sent_two))

    e_sent_six.append(joined(*joining[1], joining[1][1]))
    returned = [(sent, got, (e_sent, last)) for (sent, got, e_sent), last in zip(returned, e_sent_six)]
    kernel_grad = kernel_terms
    for step, after in zip(steps[1:], ((sent_two, sent_six), (sent_four, e_sent_two), ())):
        kernel_grad = exchanged(once(kernel_grad, *after), *step)

    wide = min(WIDE, width)
    spec = pl.BlockSpec((rows, wide), lambda h: (0, h))
    query_grad = pl.pallas_call(
        query_kernel,
        grid=(channels // wide,),
        in_specs=[
            spec,
            pl.BlockSpec((2, PAD, wide), lambda h: (0, 0, h)),
            pl.BlockSpec((3, TAPS, wide), lambda h: (0, 0, h)),
        ],
        out_specs=spec,
        out_shape=jax.ShapeDtypeStruct((rows, channels), half),
        compiler_params=pltpu.CompilerParams(vmem_limit_bytes=VMEM),
        name="query_finish",
    )(dq, q_after, conv_weight)

    lows = []
    highs = []
    for group in range(GROUPS):
        own = results[group][1]
        sent, got, e_sent = returned[group]
        low = own[:, :PAD] + jnp.where(first_core, got[0, :, :PAD].astype(f32), 0.0)
        high = own[:, HALF : HALF + PAD]
        for x in sent:
            low = low + x[:, :PAD].astype(f32)
        for x in e_sent:
            high = high + x[:, :PAD].astype(f32)
        lows.append(low)
        highs.append(high)
    after = after_rows((jnp.concatenate(lows, axis=2), jnp.concatenate(highs, axis=2)))
    outs = None
    for group in range(GROUPS):
        sent, got, e_sent = returned[group]
        outs = finished(group, heads, place, results[group][1], sent, got, e_sent, after, conv_weight, outs)
    return (query_grad[None], outs[0][None], outs[1][None], kernel_grad)


def solution(mesh):
    placed = (
        P("dp", "ctx", None),
        P("dp", "ctx", None),
        P("dp", "ctx", None),
        P(),
        P("dp", "ctx", None),
        P("dp", "ctx", None),
    )
    return jax.shard_map(
        body,
        mesh=mesh,
        in_specs=placed,
        out_specs=(P("dp", "ctx", None), P("dp", "ctx", None), P("dp", "ctx", None), P()),
        check_vma=False,
    )
```

```python
import functools
import math

import jax
import jax.numpy as jnp
from jax import lax
from jax.experimental import pallas as pl
from jax.experimental.pallas import tpu as pltpu
from jax.sharding import PartitionSpec as P

HEAD = 128
TAPS = 4
BLK = 64
BEHIND = 6
MAX_REMOTE = 2
HALF = 128
OWN_BLOCKS = 4
PAD = 8
RUN = HALF + PAD
SLOTS = BEHIND * MAX_REMOTE
KEYS = SLOTS * BLK + 2 * HALF
GROUPS = 2
HIDDEN = 1 << 30
WIDE = 512
VMEM = 48 * 1024 * 1024


def along(x, pairs):
    return lax.ppermute(x, "ctx", pairs)


def ring_pairs(count, by):
    return [(i, (i + by) % count) for i in range(count)]


def sibling_pairs(count):
    return [(i, i ^ 1) for i in range(count)]


def wrapped_out(count, by):
    return [(i, i + by - count) for i in range(count - by, count)]


def wrapped_back(count, by):
    return [(j, i) for i, j in wrapped_out(count, by)]


def once(x, *others):
    return lax.optimization_barrier((x, others))[0]


def exchange_steps(axes):
    steps = []
    for axis in axes:
        step = 1
        while step < lax.axis_size(axis):
            steps.append((axis, step))
            step *= 4
    return steps


def exchanged(x, axis, step):
    count = lax.axis_size(axis)
    others = [lax.ppermute(x, axis, [(i, i ^ (step * k)) for i in range(count)]) for k in range(1, 4)]
    return (x + others[0]) + (others[1] + others[2])


def shared(own, from_two, from_four, from_six, first_core, pairs):
    mine = jnp.stack(
        [
            jnp.where(first_core, own, from_two),
            jnp.where(first_core, from_two, from_four),
            jnp.where(first_core, from_four, from_six),
        ]
    )
    return along(mine, pairs)


def table_of_slots(lists, my_index, count):
    span = lists * BLK // HALF
    upper = span >= count
    owners = jnp.where(upper, 2 * count - 1 - span, span)
    local = jnp.where(upper, OWN_BLOCKS // 2, 0) + lists % (HALF // BLK)
    distance = ((my_index - owners) % count).reshape(-1)
    reach = BEHIND - jnp.arange(BEHIND, dtype=jnp.int32)
    block_ids = jnp.arange(OWN_BLOCKS, dtype=jnp.int32)
    wanted = jnp.any(
        (distance[:, None, None] == reach[None, :, None])
        & (local.reshape(-1)[:, None, None] == block_ids[None, None, :]),
        axis=0,
    )
    rank = jnp.cumsum(wanted.astype(jnp.int32), axis=1) - 1
    slot_ids = jnp.arange(MAX_REMOTE, dtype=jnp.int32)
    hits = wanted[:, :, None] & (rank[:, :, None] == slot_ids[None, None, :])
    chosen = jnp.sum(jnp.where(hits, block_ids[None, :, None], 0), axis=1)
    chosen_named = jnp.any(hits, axis=1)
    wraps = (reach > my_index)[:, None]
    block = jnp.where(wraps, chosen, slot_ids[None, :])
    named = jnp.where(wraps, chosen_named, wanted[:, :MAX_REMOTE])
    rows = jnp.arange(BEHIND, dtype=jnp.int32)[:, None]
    index = jnp.where(block < 2, rows * 2 + block, SLOTS + rows * 2 + block - 2)
    owner = ((my_index - reach) % count)[:, None]
    piece = jnp.where(block < 2, owner, 2 * count - 1 - owner)
    start = piece * HALF + (block % 2) * BLK
    start = jnp.where(named, start, HIDDEN)
    spread = jnp.arange(BLK, dtype=jnp.int32)
    positions = (start.reshape(-1)[:, None] + spread[None, :]).reshape(-1)
    return index.reshape(-1), positions


def attention_kernel(
    meta, key_pos, query_pos, q_raw, k_raw, v_raw, cot, weight, q_halo, far_halo, high_halo,
    two, four, six, odd, e_two, e_four, e_six, e_odd,
    dq_out, own_out, odd_out, even_out, e_odd_out, e_even_out, taps_out,
    hide, xq, xk, xv, kall, vall, kt, vt, scores, dprob, probs_half, dscore, gk, gv,
):
    my_index = meta[SLOTS]
    wrapping = my_index < BEHIND
    scale = HEAD ** -0.5
    f32 = jnp.float32
    half = jnp.bfloat16

    @pl.when(pl.program_id(0) == 0)
    def _():
        hide[...] = jnp.where(key_pos[...] <= query_pos[...], 0.0, -jnp.inf)
        gk[...] = jnp.zeros_like(gk)
        gv[...] = jnp.zeros_like(gv)

    raw = (xk, xv)
    fields = (kall, vall)
    tables = (kt, vt)
    near = {1: lambda n: odd[0, n], 3: lambda n: odd[1, n], 5: lambda n: odd[2, n],
            2: lambda n: two[n], 4: lambda n: four[n], 6: lambda n: six[n]}
    wrapped = {1: lambda n: e_odd[0, n], 3: lambda n: e_odd[1, n], 5: lambda n: e_odd[2, n],
               2: lambda n: e_two[n], 4: lambda n: e_four[n], 6: lambda n: e_six[n]}

    def convolved(x, place, which):
        base = place * RUN + PAD
        total = weight[which, 0:1, :] * x[base : base + HALF, :]
        for tap in range(1, TAPS):
            total = total + weight[which, tap : tap + 1, :] * x[base - tap : base - tap + HALF, :]
        return total.astype(half)

    def last_rows(x, place):
        return x[place * RUN + HALF : place * RUN + RUN, :]

    for side in range(2):
        xq[side * RUN : side * RUN + PAD, :] = q_halo[side]
        xq[side * RUN + PAD : (side + 1) * RUN, :] = q_raw[side * HALF : (side + 1) * HALF, :].astype(f32)
    queries = jnp.concatenate([convolved(xq, 0, 0), convolved(xq, 1, 0)], axis=0)

    own_raw = (k_raw, v_raw)
    for n in range(2):
        x = raw[n]
        for place in range(BEHIND + 1):
            base = place * RUN
            if place < BEHIND:
                rows = near[BEHIND - place](n).astype(f32)
            else:
                rows = own_raw[n][0:HALF, :].astype(f32)
            before = far_halo[n] if place == 0 else last_rows(x, place - 1)
            x[base : base + PAD, :] = jnp.where(BEHIND - place == my_index, 0.0, before)
            x[base + PAD : base + RUN, :] = rows
        base = (BEHIND + 1) * RUN
        x[base : base + PAD, :] = high_halo[n]
        x[base + PAD : base + RUN, :] = own_raw[n][HALF : 2 * HALF, :].astype(f32)
        for place in range(BEHIND):
            fields[n][place * HALF : (place + 1) * HALF, :] = convolved(x, place, n + 1)
        for side in range(2):
            first = SLOTS * BLK + side * HALF
            tables[n][first : first + HALF, :] = convolved(x, BEHIND + side, n + 1)

    @pl.when(wrapping)
    def _():
        gk[...] = jnp.zeros_like(gk)
        gv[...] = jnp.zeros_like(gv)
        for n in range(2):
            x = raw[n]
            for step in range(1, BEHIND + 1):
                place = BEHIND - step
                base = (BEHIND + 2 + place) * RUN
                before = last_rows(x, place)
                if step > 1:
                    before = jnp.where(step == my_index + 1, before, last_rows(x, BEHIND + 3 + place))
                x[base : base + PAD, :] = before
                x[base + PAD : base + RUN, :] = wrapped[step](n).astype(f32)
                first = (BEHIND + place) * HALF
                fields[n][first : first + HALF, :] = convolved(x, BEHIND + 2 + place, n + 1)

    for slot in range(SLOTS):
        source = pl.ds(pl.multiple_of(meta[slot] * BLK, BLK), BLK)
        for n in range(2):
            tables[n][slot * BLK : (slot + 1) * BLK, :] = fields[n][source, :]

    grads = cot[...]
    contract_last = (((1,), (1,)), ((), ()))
    contract_first = (((0,), (0,)), ((), ()))
    plain = (((1,), (0,)), ((), ()))
    chunk = 128
    chunks = [slice(c, c + chunk) for c in range(0, KEYS, chunk)]
    width = 2 * HALF

    def folded(x, op):
        return op(x.reshape(chunk // 8, 8, width), axis=0)

    factor = scale * math.log2(math.e)
    tops = None
    for c in chunks:
        s = lax.dot_general(kt[c, :], queries, contract_last, preferred_element_type=f32)
        s = s * factor + hide[c, :]
        scores[c, :] = s
        top = folded(s, jnp.max)
        tops = top if tops is None else jnp.maximum(tops, top)
    top = jnp.max(tops, axis=0, keepdims=True)
    totals = jnp.zeros((8, width), f32)
    for c in chunks:
        e = jnp.exp2(scores[c, :] - top)
        scores[c, :] = e
        totals = totals + folded(e, jnp.sum)
    inverse = 1.0 / jnp.sum(totals, axis=0, keepdims=True)
    deltas = jnp.zeros((8, width), f32)
    for c in chunks:
        p = scores[c, :] * inverse
        scores[c, :] = p
        pb = p.astype(half)
        probs_half[c, :] = pb
        dp = lax.dot_general(vt[c, :], grads, contract_last, preferred_element_type=f32)
        dprob[c, :] = dp
        deltas = deltas + folded(pb.astype(f32) * dp, jnp.sum)
    delta = jnp.sum(deltas, axis=0, keepdims=True)
    for number, c in enumerate(chunks):
        ds = (scores[c, :] * (dprob[c, :] - delta)).astype(half)
        dscore[c, :] = ds
        dk = lax.dot_general(ds, queries, plain, preferred_element_type=f32) * scale
        dv = lax.dot_general(probs_half[c, :], grads, plain, preferred_element_type=f32)
        for n, (out, term) in enumerate(((gk, dk), (gv, dv))):
            if c.start < SLOTS * BLK:
                for part in range(chunk // BLK):
                    slot = number * (chunk // BLK) + part
                    target = pl.ds(pl.multiple_of(meta[slot] * BLK, BLK), BLK)
                    out[target, :] = term[part * BLK : (part + 1) * BLK, :]
            else:
                first = c.start - SLOTS * BLK
                own_out[n, first : first + chunk, :] = term
    dq = lax.dot_general(dscore[...], kt[...], contract_first, preferred_element_type=f32) * scale
    dq_out[...] = dq

    def tap_sums(terms, x):
        sums = []
        for tap in range(TAPS):
            total = jnp.zeros((8, HEAD), f32)
            for rows, place in terms:
                base = place * RUN + PAD - tap
                total = total + jnp.sum((rows() * x[base : base + HALF, :]).reshape(HALF // 8, 8, HEAD), axis=0)
            sums.append(jnp.sum(total, axis=0, keepdims=True))
        return jnp.concatenate(sums, axis=0)

    taps_out[0] = tap_sums([(lambda s=s: dq_out[s * HALF : (s + 1) * HALF, :], s) for s in range(2)], xq)
    for n, g in enumerate((gk, gv)):
        terms = [(lambda p=p, g=g: g[p * HALF : (p + 1) * HALF, :], p) for p in range(BEHIND)]
        terms += [(lambda s=s, n=n: own_out[n, s * HALF : (s + 1) * HALF, :], BEHIND + s) for s in range(2)]
        taps_out[n + 1] = tap_sums(terms, raw[n])

    @pl.when(wrapping)
    def _():
        for n, g in enumerate((gk, gv)):
            terms = [
                (lambda p=p, g=g: g[(BEHIND + p) * HALF : (BEHIND + p + 1) * HALF, :], BEHIND + 2 + p)
                for p in range(BEHIND)
            ]
            taps_out[n + 1] = taps_out[n + 1] + tap_sums(terms, raw[n])

    for n, g in enumerate((gk, gv)):
        for step in range(1, BEHIND + 1):
            place = BEHIND - step
            low = g[place * HALF : (place + 1) * HALF, :]
            high = g[(BEHIND + place) * HALF : (BEHIND + place + 1) * HALF, :]
            if step % 2:
                odd_out[step // 2, n] = low.astype(half)
                e_odd_out[step // 2, n] = high.astype(half)
            else:
                even_out[step // 2 - 1, n] = low
                e_even_out[step // 2 - 1, n] = high


def attention_terms(group, heads, meta, key_pos, query_pos, tensors, weight, halos, near, wrapped):
    q_raw, k_raw, v_raw, cot = tensors
    first = group * heads
    smem = pl.BlockSpec(memory_space=pltpu.SMEM)

    def whole(shape):
        return pl.BlockSpec(shape, lambda h: (0,) * len(shape))

    def of_head(*lead):
        return pl.BlockSpec(lead + (HEAD,), lambda h: (0,) * len(lead) + (first + h,))

    def of_group(*lead):
        return pl.BlockSpec(lead + (HEAD,), lambda h: (0,) * len(lead) + (h,))

    rows = 2 * HALF
    channels = heads * HEAD
    f32 = jnp.float32
    half = jnp.bfloat16
    piece = of_group(2, HALF)
    pieces = of_group(3, 2, HALF)
    run = functools.partial(pltpu.VMEM)
    return pl.pallas_call(
        attention_kernel,
        grid=(heads,),
        in_specs=[
            smem, whole((KEYS, 1)), whole((1, rows)),
            of_head(rows), of_head(rows), of_head(rows), of_head(rows),
            of_head(3, TAPS), of_head(2, PAD), of_head(2, PAD), of_head(2, PAD),
            piece, piece, piece, pieces, piece, piece, piece, pieces,
        ],
        out_specs=[of_group(rows), of_group(2, rows), pieces, pieces, pieces, pieces, of_group(3, TAPS)],
        out_shape=[
            jax.ShapeDtypeStruct((rows, channels), f32),
            jax.ShapeDtypeStruct((2, rows, channels), f32),
            jax.ShapeDtypeStruct((3, 2, HALF, channels), half),
            jax.ShapeDtypeStruct((3, 2, HALF, channels), f32),
            jax.ShapeDtypeStruct((3, 2, HALF, channels), half),
            jax.ShapeDtypeStruct((3, 2, HALF, channels), f32),
            jax.ShapeDtypeStruct((3, TAPS, channels), f32),
        ],
        scratch_shapes=[
            run((KEYS, rows), f32),
            run((2 * RUN, HEAD), f32),
            run((14 * RUN, HEAD), f32), run((14 * RUN, HEAD), f32),
            run((2 * BEHIND * HALF, HEAD), half), run((2 * BEHIND * HALF, HEAD), half),
            run((KEYS, HEAD), half), run((KEYS, HEAD), half),
            run((KEYS, rows), f32), run((KEYS, rows), f32),
            run((KEYS, rows), half), run((KEYS, rows), half),
            run((2 * BEHIND * HALF, HEAD), f32), run((2 * BEHIND * HALF, HEAD), f32),
        ],
        compiler_params=pltpu.CompilerParams(vmem_limit_bytes=VMEM),
        cost_estimate=pl.CostEstimate(
            flops=heads * 100 * rows * KEYS * HEAD, bytes_accessed=heads * 3 * 1024 * 1024, transcendentals=heads * rows * KEYS
        ),
        name="attention",
    )(meta, key_pos, query_pos, q_raw, k_raw, v_raw, cot, weight, *halos, *near, *wrapped)


def unconvolved(rows, after, taps):
    extended = jnp.concatenate([rows, after], axis=0)
    total = taps[0:1, :] * extended[:HALF, :]
    for tap in range(1, TAPS):
        total = total + taps[tap : tap + 1, :] * extended[tap : tap + HALF, :]
    return total.astype(jnp.bfloat16)


def query_kernel(grad, after, weight, out):
    for side in range(2):
        rows = slice(side * HALF, (side + 1) * HALF)
        out[rows, :] = unconvolved(grad[rows, :], after[side], weight[0])


def final_kernel(terms, meta, own, beside, after, weight, *rest):
    outs = rest[-2:]
    sent = rest[:terms]
    e_sent = rest[terms : terms + 2]
    f32 = jnp.float32
    first_core = meta[0] % 2 == 0
    for n in range(2):
        low = own[n, 0:HALF, :] + jnp.where(first_core, beside[0, n].astype(f32), 0.0)
        for x in sent:
            low = low + x[n].astype(f32)
        high = own[n, HALF : 2 * HALF, :]
        for x in e_sent:
            high = high + x[n].astype(f32)
        outs[n][0:HALF, :] = unconvolved(low, after[n, 0], weight[n + 1])
        outs[n][HALF : 2 * HALF, :] = unconvolved(high, after[n, 1], weight[n + 1])


def combine_kernel(meta, even, odd, e_even, e_odd, two, four, six, e_two, e_four, e_six):
    f32 = jnp.float32
    first_core = meta[0] % 2 == 0
    for evens, odds, outs in ((even, odd, (two, four, six)), (e_even, e_odd, (e_two, e_four, e_six))):
        for n in range(2):
            wide = [odds[m, n].astype(f32) for m in range(3)]
            beside = [
                jnp.where(first_core, wide[1], wide[0]),
                jnp.where(first_core, wide[2], wide[1]),
                jnp.where(first_core, 0.0, wide[2]),
            ]
            for m, out in enumerate(outs):
                out[n] = (evens[m, n] + beside[m]).astype(out.dtype)


def combined(meta, even, odd, e_even, e_odd):
    channels = even.shape[-1]
    wide = min(WIDE, channels)
    half = jnp.bfloat16
    f32 = jnp.float32
    pieces = pl.BlockSpec((3, 2, HALF, wide), lambda h: (0, 0, 0, h))
    piece = pl.BlockSpec((2, HALF, wide), lambda h: (0, 0, h))
    types = [f32] + [half] * 4 + [f32]
    return pl.pallas_call(
        combine_kernel,
        grid=(channels // wide,),
        in_specs=[pl.BlockSpec(memory_space=pltpu.SMEM)] + [pieces] * 4,
        out_specs=[piece] * 6,
        out_shape=[jax.ShapeDtypeStruct((2, HALF, channels), t) for t in types],
        compiler_params=pltpu.CompilerParams(vmem_limit_bytes=VMEM),
        name="combine",
    )(meta, even, odd, e_even, e_odd)


def finished(group, heads, meta, own, near, beside, wrapped, after, weight, earlier):
    rows = 2 * HALF
    channels = heads * HEAD
    wide = min(WIDE, channels)
    first = group * (channels // wide)

    def of_group(*lead):
        return pl.BlockSpec(lead + (wide,), lambda h: (0,) * len(lead) + (h,))

    def of_head(*lead):
        return pl.BlockSpec(lead + (wide,), lambda h: (0,) * len(lead) + (first + h,))

    piece = of_group(2, HALF)
    anywhere = pl.BlockSpec(memory_space=pl.ANY)
    shape = jax.ShapeDtypeStruct((rows, GROUPS * channels), jnp.bfloat16)
    extra = [] if earlier is None else list(earlier)
    terms = len(near) + len(wrapped)
    return pl.pallas_call(
        functools.partial(final_kernel, len(near)),
        grid=(channels // wide,),
        in_specs=[
            pl.BlockSpec(memory_space=pltpu.SMEM), of_group(2, rows), of_group(1, 2, HALF),
            of_head(2, 2, PAD), of_head(3, TAPS),
        ]
        + [piece] * terms
        + [anywhere] * len(extra),
        out_specs=[of_head(rows), of_head(rows)],
        out_shape=[shape, shape],
        input_output_aliases={5 + terms + n: n for n in range(len(extra))},
        compiler_params=pltpu.CompilerParams(vmem_limit_bytes=VMEM),
        name="finish",
    )(meta, own, beside, after, weight, *near, *wrapped, *extra)


def body(query_in, key_in, value_in, conv_weight, out_grad, block_lists):
    q_raw, k_raw, v_raw, cot = (x[0] for x in (query_in, key_in, value_in, out_grad))
    f32 = jnp.float32
    half = jnp.bfloat16
    channels = q_raw.shape[1]
    rows = 2 * HALF
    heads = channels // HEAD // GROUPS
    width = heads * HEAD
    count = lax.axis_size("ctx")
    my_index = lax.axis_index("ctx")
    first_core = my_index % 2 == 0
    is_last = my_index == count - 1
    up = [(i, i + 1) for i in range(count - 1)]
    down = [(i + 1, i) for i in range(count - 1)]
    every = sibling_pairs(count)
    few = sibling_pairs(BEHIND)

    tail = slice(HALF - PAD, HALF)
    high_tail = slice(rows - PAD, rows)
    q_before = along(q_raw[tail], up)
    far = along(jnp.stack([k_raw[tail], v_raw[tail]]), ring_pairs(count, BEHIND + 1))
    above = along(jnp.stack([x[high_tail] for x in (q_raw, k_raw, v_raw)]), down)

    near = []
    wrapped = []
    for group in range(GROUPS):
        part = slice(group * width, (group + 1) * width)
        low = jnp.stack([k_raw[:HALF, part], v_raw[:HALF, part]])
        high = jnp.stack([k_raw[HALF:, part], v_raw[HALF:, part]])
        if group:
            low, high = once((low, high), ready)
        two = along(low, ring_pairs(count, 2))
        six = along(low, ring_pairs(count, 6))
        if group == 0:
            ready = once(six, q_before, far, above)
            four = along(ready, ring_pairs(count, -2))
        else:
            four = along(low, ring_pairs(count, 4))
        e_two = along(high, wrapped_out(count, 2))
        e_six = along(high, wrapped_out(count, 6))
        near.append((two, four, six, low))
        wrapped.append((e_two, e_six, high))

    below = jnp.stack([x[tail] for x in (q_raw, k_raw, v_raw)])
    above = jnp.where(is_last, below, above).astype(f32)
    q_halo = jnp.stack([q_before.astype(f32), above[0]])
    halos = (q_halo, far.astype(f32), above[1:])

    index, remote_pos = table_of_slots(block_lists[0], my_index, count)
    spread = jnp.arange(HALF, dtype=jnp.int32)
    positions = jnp.concatenate([my_index * HALF + spread, (2 * count - 1 - my_index) * HALF + spread])
    key_pos = jnp.concatenate([remote_pos, positions])[:, None]
    place = my_index[None].astype(jnp.int32)
    meta = jnp.concatenate([index, place]).astype(jnp.int32)

    def after_rows(heads_of):
        low, high = heads_of
        next_low = along(low, down)
        next_high = along(high, up)
        return jnp.stack([jnp.where(is_last, high, next_low), next_high], axis=-3)

    steps = exchange_steps(("ctx", "dp"))
    results = []
    returned = []
    joining = []

    def joined(two, four, e_six, e_four, after):
        four, e_four = once((four, e_four), after)
        sent_two = along((two + four.astype(f32)).astype(half), ring_pairs(count, -2))
        return sent_two, along((e_six + e_four.astype(f32)).astype(half), wrapped_back(count, 6))

    for group in range(GROUPS):
        two, four, six, low = near[group]
        e_two, e_six, high = wrapped[group]
        if group:
            low, high, e_six = once((low, high, e_six), results[-1][6])
        else:
            low, high = once((low, high), near[1][0])
        e_four = along(e_six, [(i + 2, i) for i in range(4)])
        beside = shared(low, two, four, six, first_core, every)
        e_beside = shared(high, e_two, e_four, e_six, first_core, few)
        result = attention_terms(
            group, heads, meta, key_pos, positions[None, :], (q_raw, k_raw, v_raw, cot), conv_weight, halos,
            (two, four, six, beside), (e_two, e_four, e_six, e_beside),
        )
        _, _, odd, even, e_odd, e_even, _ = result
        if group:
            last_sent = [joined(*joining[0], result[6])]
            odd, e_odd = once((odd, e_odd), returned[-1][0], returned[-1][2], joining[0][1], joining[0][3])
        got = along(odd, every)
        e_got = along(e_odd, few)
        if group:
            kernel_terms = exchanged(jnp.concatenate([r[6] for r in (*results, result)], axis=2), *steps[0])
            dq = jnp.concatenate([r[0] for r in (*results, result)], axis=1)
            q_after = after_rows((dq[:PAD], dq[HALF : HALF + PAD]))
            got, e_got = once((got, e_got), kernel_terms, q_after)
        two, four, six, e_two, e_four, e_six = combined(place, even, got, e_even, e_got)
        meta = once(meta, two)
        passed = along(four, ring_pairs(count, -2))
        sent_six = along(six, ring_pairs(count, -6))
        e_sent_two = along(e_two, wrapped_back(count, 2))
        joining.append((two, passed, e_six, along(e_four, [(i, i + 2) for i in range(4)])))
        results.append(result)
        returned.append((sent_six, got, e_sent_two))

    last_sent.append(joined(*joining[1], e_sent_two))
    returned = [((sent, two), got, (e_sent, six)) for (sent, got, e_sent), (two, six) in zip(returned, last_sent)]
    kernel_grad = kernel_terms
    for step, after in zip(steps[1:], ((passed, sent_six), (last_sent[0][0], e_sent_two), ())):
        kernel_grad = exchanged(once(kernel_grad, *after), *step)

    wide = min(WIDE, width)
    spec = pl.BlockSpec((rows, wide), lambda h: (0, h))
    query_grad = pl.pallas_call(
        query_kernel,
        grid=(channels // wide,),
        in_specs=[
            spec,
            pl.BlockSpec((2, PAD, wide), lambda h: (0, 0, h)),
            pl.BlockSpec((3, TAPS, wide), lambda h: (0, 0, h)),
        ],
        out_specs=spec,
        out_shape=jax.ShapeDtypeStruct((rows, channels), half),
        compiler_params=pltpu.CompilerParams(vmem_limit_bytes=VMEM),
        name="query_finish",
    )(dq, q_after, conv_weight)

    lows = []
    highs = []
    for group in range(GROUPS):
        own = results[group][1]
        sent, got, e_sent = returned[group]
        low = own[:, :PAD] + jnp.where(first_core, got[0, :, :PAD].astype(f32), 0.0)
        high = own[:, HALF : HALF + PAD]
        for x in sent:
            low = low + x[:, :PAD].astype(f32)
        for x in e_sent:
            high = high + x[:, :PAD].astype(f32)
        lows.append(low)
        highs.append(high)
    after = after_rows((jnp.concatenate(lows, axis=2), jnp.concatenate(highs, axis=2)))
    outs = None
    for group in range(GROUPS):
        sent, got, e_sent = returned[group]
        outs = finished(group, heads, place, results[group][1], sent, got, e_sent, after, conv_weight, outs)
    return (query_grad[None], outs[0][None], outs[1][None], kernel_grad)


def solution(mesh):
    placed = (
        P("dp", "ctx", None),
        P("dp", "ctx", None),
        P("dp", "ctx", None),
        P(),
        P("dp", "ctx", None),
        P("dp", "ctx", None),
    )
    return jax.shard_map(
        body,
        mesh=mesh,
        in_specs=placed,
        out_specs=(P("dp", "ctx", None), P("dp", "ctx", None), P("dp", "ctx", None), P()),
        check_vma=False,
    )
```
